128 devices in a mesh: grp: 8 (over x, core), mem: 16 (over z, y).
Axes of the slice: x: 4, y: 4, z: 4, core: 2. Of those that a mesh axis runs over, the one named last changes fastest.
Arguments:
- embeddings: bfloat16 [131072, 768], P(('grp', 'mem'))
- cluster: int32 [131072], P(('grp', 'mem')), may hold values from -1 to 15, as said below
- rank: int32 [131072], P(('grp', 'mem')), may hold values from -1 to 8191, as said below
Outputs:
- best_match: float32 [131072], P(('grp', 'mem'))
The draws below stay inside these ranges and needn't reach their ends.
Inputs may be any that keep to these rules, and one draw needn't show every extreme that they name: cluster is -1 exactly where rank is -1. Ranks are distinct within a cluster; among the rows of one device, at most 4 have the same cluster // 2 and the same rank // 256, and every device reaches 4 for some such pair.
All inputs are finite; a program needn't handle non-finite values.
Results may differ from the reference program's by a relative error of at most 0.0004.
Values may be sent and summed in bfloat16 or wider, within the bound.
A program may use at most 128 MiB of HBM per device.

```python
import math
import jax
import jax.numpy as jnp
from jax import lax

D = 768
CLUS_GRP = 2
ROWS_DEV = 1024
ROWS = 131072
CLUSTERS = 16
CAP = 8192
HALF = 256
QH = 4
PROTOS = 1024
N_GRP = 8
N_MEM = 16
DEVICES = 128


def layout_draw(key):
    base = jax.random.fold_in(key, 7)
    keys = jax.random.split(base, 5)
    units = N_GRP * 2 * N_MEM
    unit_slots = CLUS_GRP * HALF
    counts = jax.random.randint(keys[0], (DEVICES, units), QH - QH // 2, QH + 1)
    sources = jnp.arange(DEVICES)
    first = jax.random.randint(keys[1], (DEVICES,), 0, DEVICES)
    unit_a = first // N_MEM * 2 * N_MEM + 2 * (first % N_MEM)
    counts = counts.at[sources, unit_a].set(QH)
    counts = counts.at[sources, unit_a + 1].set(QH)
    second = jax.random.randint(keys[2], (DEVICES,), 0, DEVICES)
    unit_c = second // N_MEM * 2 * N_MEM + second % N_MEM
    unit_d = second // N_MEM * 2 * N_MEM + 2 * N_MEM - 1 - second % N_MEM
    counts = counts.at[sources, unit_c].set(QH)
    counts = counts.at[sources, unit_d].set(QH)
    inclusive = jnp.cumsum(counts, axis=1)
    exclusive = inclusive - counts
    spots = jnp.arange(ROWS_DEV)
    target = jnp.sum((inclusive[:, None, :] <= spots[None, :, None]).astype(jnp.int32), axis=2)
    alive = target < units
    clipped = jnp.minimum(target, units - 1)
    within = spots[None, :] - jnp.take_along_axis(exclusive, clipped, axis=1)
    arrival = jnp.cumsum(counts, axis=0) - counts
    order = jnp.take_along_axis(arrival, clipped, axis=1) + within
    slot = jnp.clip(order, 0, unit_slots - 1)
    group_id = clipped // (2 * N_MEM)
    half_id = clipped % (2 * N_MEM)
    cluster = group_id * CLUS_GRP + slot // HALF
    rank = half_id * HALF + slot % HALF
    cluster = jnp.where(alive, cluster, -1)
    rank = jnp.where(alive, rank, -1)
    mixing = jax.vmap(lambda k: jax.random.permutation(k, ROWS_DEV))(jax.random.split(keys[4], DEVICES))
    cluster = jnp.take_along_axis(cluster, mixing, axis=1).reshape(-1)
    rank = jnp.take_along_axis(rank, mixing, axis=1).reshape(-1)
    return (cluster.astype(jnp.int32), rank.astype(jnp.int32))


def draw_cluster(key, part):
    return layout_draw(key)[0]


def draw_rank(key, part):
    return layout_draw(key)[1]


def draw_embeddings(key, part):
    cluster, rank = layout_draw(key)
    keys = jax.random.split(jax.random.fold_in(key, 11), 6)
    safe = jnp.maximum(cluster, 0)
    centers = jax.random.normal(keys[0], (CLUSTERS, D), jnp.float32)
    protos = jax.random.normal(keys[1], (CLUSTERS, PROTOS, D), jnp.float32)
    which = jax.random.randint(keys[2], (ROWS,), 0, PROTOS)
    noise = jax.random.normal(keys[3], (ROWS, D), jnp.float32)
    spread = jnp.exp(jax.random.uniform(keys[4], (ROWS, 1), jnp.float32, jnp.log(0.15), jnp.log(0.8)))
    size = jnp.exp(jax.random.uniform(keys[5], (ROWS, 1), jnp.float32, jnp.log(0.5), jnp.log(4.0)))
    values = (0.5 * centers[safe] + protos[safe, which] + spread * noise) * size
    return values.astype(jnp.bfloat16)


def setup_inputs(seed: int = 0) -> dict:
    key_list = jax.random.split(jax.random.key(seed), 4)
    return {
        "embeddings": draw_embeddings(jax.random.fold_in(key_list[3], 71), 0),
        "cluster": draw_cluster(jax.random.fold_in(key_list[3], 71), 0),
        "rank": draw_rank(jax.random.fold_in(key_list[3], 71), 0),
    }


def unit_rows(embeddings):
    wide = embeddings.astype(jnp.float32)
    total = lax.optimization_barrier(jnp.sum(wide * wide, axis=1, keepdims=True))
    return (wide * lax.rsqrt(total + 1e-06)).astype(jnp.bfloat16)

def reference(embeddings, cluster, rank):
    unit = unit_rows(embeddings)
    alive = cluster >= 0
    flat = jnp.where(alive, jnp.maximum(cluster, 0) * CAP + jnp.maximum(rank, 0), CLUSTERS * CAP).astype(jnp.int32)
    grid = jnp.zeros((CLUSTERS * CAP + 1, D), jnp.bfloat16).at[flat].set(unit)[:-1].reshape(CLUSTERS, CAP, D)
    present = jnp.zeros((CLUSTERS * CAP + 1,), jnp.int32).at[flat].set(1)[:-1].reshape(CLUSTERS, CAP)
    block = math.gcd(CAP, 512)

    def per_cluster(operands):
        table, live = operands

        def per_block(index):
            rows = lax.dynamic_slice_in_dim(table, index * block, block, 0)
            sims = jnp.dot(rows, table.T, preferred_element_type=jnp.float32)
            row_rank = index * block + jnp.arange(block, dtype=jnp.int32)
            col_rank = jnp.arange(CAP, dtype=jnp.int32)
            keep = (col_rank[None, :] < row_rank[:, None]) & (live[None, :] > 0)
            return lax.optimization_barrier(jnp.max(jnp.where(keep, sims, jnp.float32(-1.0)), axis=1))
        return lax.map(per_block, jnp.arange(CAP // block, dtype=jnp.int32)).reshape(CAP)
    best = lax.map(per_cluster, (grid, present)).reshape(-1)
    picked = best[jnp.minimum(flat, CLUSTERS * CAP - 1)]
    return jnp.where(alive, picked, jnp.float32(-1.0))
```

```python
import functools

import jax
import jax.numpy as jnp
from jax import lax
from jax.experimental import pallas as pl
from jax.experimental.pallas import tpu as pltpu
from jax.sharding import PartitionSpec as P

MESH = pl.DeviceIdType.MESH
D = 768
WIDE = 896
ROWS = 1024
HALF = 256
DEVS = 128
BF = jnp.bfloat16
F32 = jnp.float32
I32 = jnp.int32

BLOCKS = ((0, 1), (0, 1), (0, 2), (0, 3), (1, 2), (1, 3), (2, 3), (2, 3))
SHARERS = ((0, 1, 2, 3), (0, 1, 4, 5), (2, 4, 6, 7), (3, 5, 6, 7))
PLACE = ((3, 1, 1), (3, 0, 1), (0, 1, 1), (2, 0, 1), (0, 1, 0), (2, 0, 0), (1, 1, 0), (1, 0, 0))


def pick(index, table):
    out = jnp.int32(table[0])
    for at, value in enumerate(table):
        if at:
            out = jnp.where(index == at, jnp.int32(value), out)
    return out


def pick_vec(index, table):
    out = jnp.full_like(index, table[0])
    for at, value in enumerate(table):
        if at:
            out = jnp.where(index == at, jnp.int32(value), out)
    return out


def device_of(g, k, core):
    x = pick(k, [p[0] for p in PLACE])
    y = lax.rem(pick(k, [p[1] for p in PLACE]) + lax.div(g, 2), 4)
    z = lax.rem(pick(k, [p[2] for p in PLACE]) + lax.rem(lax.div(g, 2), 2) + 2 * lax.rem(g, 2), 4)
    return 2 * x + core, 4 * z + y


def my_place():
    grp, mem = lax.axis_index("grp"), lax.axis_index("mem")
    x, core = lax.div(grp, 2), lax.rem(grp, 2)
    z, y = lax.div(mem, 4), lax.rem(mem, 4)
    odd = lax.rem(y + z, 2)
    k = pick(2 * x + odd, [2, 4, 7, 6, 5, 3, 0, 1])
    gy = lax.rem(y - pick(k, [p[1] for p in PLACE]) + 4, 4)
    gz = lax.rem(z - pick(k, [p[2] for p in PLACE]) - lax.rem(gy, 2) + 8, 4)
    return grp, mem, 2 * gy + lax.div(gz, 2), k, core


FLAT_SHARERS = [k for row in SHARERS for k in row]
FLAT_POS = [BLOCKS[k].index(b) for b in range(4) for k in SHARERS[b]]
FLAT_BLOCKS = [b for pair in BLOCKS for b in pair]
FLAT_TURN = [SHARERS[BLOCKS[k][p]].index(k) for k in range(8) for p in range(2)]

NT = (((1,), (1,)), ((), ()))
NN = (((1,), (0,)), ((), ()))


def mm(a, b, dims=NN):
    return lax.dot_general(a, b, dims, preferred_element_type=F32)


def kernel(emb_ref, clu_ref, rank_ref, out_ref, unit, packed, arrived, split, held, acc, pbest,
           rbest, rep, back, send0, recv0, send1, recv1, send2, recv2, send3, recv3):
    grp, mem, g, k, core = my_place()
    me = grp * 16 + mem

    barrier = pltpu.get_barrier_semaphore()

    @pl.loop(1, DEVS)
    def _(j):
        d = lax.rem(me + j, DEVS)
        pl.semaphore_signal(barrier, inc=1, device_id=(lax.div(d, 16), lax.rem(d, 16)), device_id_type=MESH)

    @pl.loop(0, 4)
    def _(i):
        rows = pl.ds(pl.multiple_of(i * 256, 256), 256)
        wide = emb_ref[rows, :].astype(F32)
        total = jnp.sum(wide * wide, axis=1, keepdims=True)
        unit[rows, :] = (wide * lax.rsqrt(total + 1e-06)).astype(BF)

    clu, rank = clu_ref[...], rank_ref[...]
    alive = clu >= 0
    vg = clu >> 1
    vh = rank >> 8
    share = ((vh >> 3) << 2) + ((vh & 7) >> 1)
    vk = pick_vec(share, FLAT_SHARERS)
    vp = pick_vec(share, FLAT_POS)
    vx = pick_vec(vk, [p[0] for p in PLACE])
    vy = (pick_vec(vk, [p[1] for p in PLACE]) + (vg >> 1)) & 3
    vz = (pick_vec(vk, [p[2] for p in PLACE]) + ((vg >> 1) & 1) + 2 * (vg & 1)) & 3
    vdev = (2 * vx + (vh & 1)) * 16 + 4 * vz + vy
    bucket = jnp.where(alive, 2 * vdev + vp, -1)
    low = lax.broadcasted_iota(I32, (128, 256), 0)
    col = lax.broadcasted_iota(I32, (128, 256), 1)
    tri = jnp.where((low < col) | (col >= 128), 1.0, 0.0).astype(BF)
    carry = jnp.zeros((256, 128), F32)
    bid = lax.broadcasted_iota(I32, (256, 128), 0)
    spots = []
    for i in range(8):
        hit = bid == bucket[:, i * 128 : (i + 1) * 128]
        counts = mm(jnp.where(hit, 1.0, 0.0).astype(BF), tri)
        spots.append(jnp.sum(jnp.where(hit, counts[:, :128] + carry, 0.0), axis=0, keepdims=True))
        carry = carry + counts[:, 128:]
    spot = jnp.concatenate(spots, axis=1).astype(I32)
    send_at = jnp.where(alive, bucket * 4 + spot, -1)

    kind = lax.broadcasted_iota(I32, (128, ROWS), 0)
    labels = jnp.where(
        kind == 0, (rank & 255).astype(F32), jnp.where(kind == 1, (clu & 1).astype(F32), jnp.where(kind == 2, 1.0, 0.0))
    ).astype(BF)

    @pl.loop(0, 4)
    def _(i):
        line = lax.broadcasted_iota(I32, (256, ROWS), 0) + i * 256
        where_to = jnp.where(line == send_at, 1.0, 0.0).astype(BF)
        devs = pl.ds(pl.multiple_of(i * 32, 32), 32)
        packed[devs, :, 0:D] = mm(where_to, unit[...]).reshape(32, 8, D).astype(BF)
        packed[devs, :, D:WIDE] = mm(where_to, labels, NT).reshape(32, 8, 128).astype(BF)

    pl.semaphore_wait(barrier, DEVS - 1)

    pltpu.make_async_copy(packed.at[me], arrived.at[me], recv0).start()

    @pl.loop(1, DEVS)
    def _(j):
        d = lax.rem(me + 37 * j, DEVS)
        pltpu.make_async_remote_copy(
            src_ref=packed.at[d], dst_ref=arrived.at[me], send_sem=send0, recv_sem=recv0,
            device_id=(lax.div(d, 16), lax.rem(d, 16)), device_id_type=MESH,
        ).start()

    acc[...] = jnp.full(acc.shape, -1.0, F32)
    pltpu.make_async_copy(arrived, arrived, recv0).wait()

    got = arrived[...].reshape(ROWS, WIDE)
    got_labels = got[:, D:WIDE]
    lane = lax.broadcasted_iota(I32, (8, 128), 1)
    weigh = jnp.where(lane == 0, 1.0, jnp.where(lane == 1, 256.0, jnp.where(lane == 2, 2048.0, 0.0))).astype(BF)
    slot_row = mm(weigh, got_labels, NT)[0:1, :].astype(I32)
    arr_i = lax.broadcasted_iota(I32, (1, ROWS), 1)
    slot_row = jnp.where(slot_row >= 2048, slot_row - 2048 + ((arr_i >> 2) & 1) * 512, -1)
    first = lax.broadcasted_iota(I32, (256, 128), 1) == 0

    for b in range(2):
        block = pick(2 * k + b, FLAT_BLOCKS)
        turn = pick(2 * k + b, FLAT_TURN)
        for c in range(2):
            n = 2 * b + c
            line = lax.broadcasted_iota(I32, (256, ROWS), 0) + n * 256
            where_to = jnp.where(line == slot_row, 1.0, 0.0).astype(BF)
            rows = mm(where_to, got)
            here = rows[:, D + 2 : D + 3]
            split[n, :, 0:128] = jnp.where(first & (here < 0.5), 256.0, rows[:, 0:128]).astype(BF)
            split[n, :, 128:D] = rows[:, 128:D].astype(BF)
            for t in range(4):
                other = pick(4 * block + t, FLAT_SHARERS)
                pos = pick(4 * block + t, FLAT_POS)
                mine = (other == k) & (core == c)

                @pl.when(mine)
                def _():
                    pltpu.make_async_copy(split.at[n], held.at[pos, 2 * turn + core], recv1.at[pos, 2 * turn + core]).start()

                @pl.when(jnp.logical_not(mine))
                def _():
                    pltpu.make_async_remote_copy(
                        src_ref=split.at[n], dst_ref=held.at[pos, 2 * turn + core], send_sem=send1.at[n, t],
                        recv_sem=recv1.at[pos, 2 * turn + core], device_id=device_of(g, other, c), device_id_type=MESH,
                    ).start()

    @pl.loop(0, 16)
    def _(i):
        p, s = lax.div(i, 8), lax.rem(i, 8)
        pltpu.make_async_copy(held.at[p, s], held.at[p, s], recv1.at[p, s]).wait()

    diagonal = (k == 1) | (k == 7)
    probe = jnp.where(lax.broadcasted_iota(I32, (8, D), 1) == 0, 1.0, 0.0).astype(BF)

    def bias_of(cols):
        mark = mm(probe, cols, NT)[0:1, :]
        return jnp.where(mark > 2.0, -1e4, 0.0)

    @pl.when(jnp.logical_not(diagonal))
    def _():
        @pl.loop(0, 8)
        def _(b):
            cols = held[0, b]
            bias = bias_of(cols)

            @pl.loop(0, 8)
            def _(a):
                sims = mm(held[1, a], cols, NT) + bias
                acc[1, a] = jnp.maximum(acc[1, a], jnp.maximum(sims[:, :128], sims[:, 128:]))

    @pl.when(diagonal)
    def _():
        for p in range(2):
            @pl.loop(0, 8)
            def _(b):
                cols = held[p, b]
                bias = bias_of(cols)
                ri = lax.broadcasted_iota(I32, (256, 256), 0)
                ci = lax.broadcasted_iota(I32, (256, 256), 1)

                @pl.loop(b, 8)
                def _(a):
                    sims = mm(held[p, a], cols, NT) + bias
                    sims = jnp.where(ci + (b - a) * 256 < ri, sims, -1.0)
                    acc[p, a] = jnp.maximum(acc[p, a], jnp.maximum(sims[:, :128], sims[:, 128:]))

    for p in range(2):
        block = pick(2 * k + p, FLAT_BLOCKS)
        turn = pick(2 * k + p, FLAT_TURN)

        @pl.loop(0, 8)
        def _(a):
            pbest[p, a] = jnp.max(acc[p, a].T, axis=0, keepdims=True)

        for t in range(4):
            other = pick(4 * block + t, FLAT_SHARERS)
            pos = pick(4 * block + t, FLAT_POS)
            for c in range(2):
                mine = (other == k) & (core == c)

                @pl.when(mine)
                def _():
                    pltpu.make_async_copy(pbest.at[p, 2 * t + c], rbest.at[pos, core, turn], recv2.at[pos, core, turn]).start()

                @pl.when(jnp.logical_not(mine))
                def _():
                    pltpu.make_async_remote_copy(
                        src_ref=pbest.at[p, 2 * t + c], dst_ref=rbest.at[pos, core, turn], send_sem=send2.at[p, t, c],
                        recv_sem=recv2.at[pos, core, turn], device_id=device_of(g, other, c), device_id_type=MESH,
                    ).start()

    wi = lax.broadcasted_iota(I32, (128, 128), 0)
    weights = jnp.where(wi == 0, 1.0, jnp.where(wi == 1, 256.0, jnp.where(wi == 2, 2048.0, 0.0))).astype(BF)
    slot_all = mm(arrived[...].reshape(ROWS, WIDE)[:, D:WIDE], weights).astype(I32)
    sub = lax.broadcasted_iota(I32, (ROWS, 128), 0) & 7
    lanes = lax.broadcasted_iota(I32, (ROWS, 128), 1)
    slot_all = jnp.where(slot_all >= 2048, slot_all - 2048 + (sub >> 2) * 512, -1)

    @pl.loop(0, 16)
    def _(i):
        p, c, t = lax.div(i, 8), lax.rem(lax.div(i, 4), 2), lax.rem(i, 4)
        pltpu.make_async_copy(rbest.at[p, c, t], rbest.at[p, c, t], recv2.at[p, c, t]).wait()

    value = jnp.full((ROWS, 128), -1.0, F32)
    for b in range(2):
        for c in range(2):
            best = jnp.maximum(
                jnp.maximum(rbest[b, c, 0], rbest[b, c, 1]), jnp.maximum(rbest[b, c, 2], rbest[b, c, 3])
            )
            for e in range(2):
                at = lanes + (b * 512 + c * 256 + e * 128)
                value = jnp.where(slot_all == at, best[:, e * 128 : (e + 1) * 128], value)
    value = jnp.max(value, axis=1, keepdims=True)
    value = jnp.where(lanes == sub, value, -1.0).reshape(DEVS, 8, 128)
    rep[...] = jnp.max(value, axis=1, keepdims=True)

    pltpu.make_async_copy(rep.at[me], back.at[me], recv3).start()

    @pl.loop(1, DEVS)
    def _(j):
        d = lax.rem(me + 37 * j, DEVS)
        pltpu.make_async_remote_copy(
            src_ref=rep.at[d], dst_ref=back.at[me], send_sem=send3, recv_sem=recv3,
            device_id=(lax.div(d, 16), lax.rem(d, 16)), device_id_type=MESH,
        ).start()

    pltpu.make_async_copy(back, back, recv3).wait()
    mine = jnp.broadcast_to(back[...], (DEVS, 8, 128)).reshape(ROWS, 128)
    mine = jnp.max(jnp.where(lanes == sub, mine, -1.0), axis=1, keepdims=True)
    line = lax.broadcasted_iota(I32, (ROWS, 128), 0)
    for i in range(8):
        part = slice(i * 128, (i + 1) * 128)
        out_ref[:, part] = jnp.max(jnp.where(line == send_at[:, part], mine, -1.0), axis=0, keepdims=True)

    some = packed.at[pl.ds(0, DEVS - 1)]
    pltpu.make_async_copy(some, some, send0).wait()
    some = rep.at[pl.ds(0, DEVS - 1)]
    pltpu.make_async_copy(some, some, send3).wait()
    for b in range(2):
        block = pick(2 * k + b, FLAT_BLOCKS)
        for t in range(4):
            other = pick(4 * block + t, FLAT_SHARERS)
            for c in range(2):
                @pl.when(jnp.logical_not((other == k) & (core == c)))
                def _():
                    pltpu.make_async_copy(split.at[2 * b + c], split.at[2 * b + c], send1.at[2 * b + c, t]).wait()
                    pltpu.make_async_copy(pbest.at[b, 2 * t + c], pbest.at[b, 2 * t + c], send2.at[b, t, c]).wait()


def on_device(embeddings, cluster, rank):
    vmem = pl.BlockSpec(memory_space=pltpu.VMEM)
    out = pl.pallas_call(
        kernel,
        out_shape=jax.ShapeDtypeStruct((1, ROWS), F32),
        in_specs=[vmem] * 3,
        out_specs=vmem,
        scratch_shapes=[
            pltpu.VMEM((ROWS, D), BF),
            pltpu.VMEM((DEVS, 8, WIDE), BF),
            pltpu.VMEM((DEVS, 8, WIDE), BF),
            pltpu.VMEM((4, HALF, D), BF),
            pltpu.VMEM((2, 8, HALF, D), BF),
            pltpu.VMEM((2, 8, HALF, 128), F32),
            pltpu.VMEM((2, 8, 1, HALF), F32),
            pltpu.VMEM((2, 2, 4, 1, HALF), F32),
            pltpu.VMEM((DEVS, 1, 128), F32),
            pltpu.VMEM((DEVS, 1, 128), F32),
            pltpu.SemaphoreType.DMA,
            pltpu.SemaphoreType.DMA,
            pltpu.SemaphoreType.DMA((4, 4)),
            pltpu.SemaphoreType.DMA((2, 8)),
            pltpu.SemaphoreType.DMA((2, 4, 2)),
            pltpu.SemaphoreType.DMA((2, 2, 4)),
            pltpu.SemaphoreType.DMA,
            pltpu.SemaphoreType.DMA,
        ],
        compiler_params=pltpu.CompilerParams(
            collective_id=0, has_side_effects=True, vmem_limit_bytes=56 * 2**20
        ),
        cost_estimate=pl.CostEstimate(flops=12_000_000_000, bytes_accessed=2_000_000, transcendentals=1024),
    )(embeddings, cluster.reshape(1, -1), rank.reshape(1, -1))
    return out.reshape(-1)


def solution(mesh):
    in_specs = (P(("grp", "mem"), None), P(("grp", "mem")), P(("grp", "mem")))
    out_specs = P(("grp", "mem"))
    return jax.shard_map(
        on_device, mesh=mesh, in_specs=in_specs, out_specs=out_specs, check_vma=False
    )
```

```python
import functools

import jax
import jax.numpy as jnp
from jax import lax
from jax.experimental import pallas as pl
from jax.experimental.pallas import tpu as pltpu
from jax.sharding import PartitionSpec as P

MESH = pl.DeviceIdType.MESH
D = 768
WIDE = 896
ROWS = 1024
HALF = 256
DEVS = 128
BF = jnp.bfloat16
F32 = jnp.float32
I32 = jnp.int32

BLOCKS = ((0, 1), (0, 1), (0, 2), (1, 2), (0, 3), (1, 3), (2, 3), (2, 3))
SHARERS = ((0, 1, 2, 4), (0, 1, 3, 5), (2, 3, 6, 7), (4, 5, 6, 7))
PLACE = ((1, 1, 0), (0, 2, 1), (2, 1, 1), (3, 1, 2), (1, 2, 0), (0, 1, 1), (2, 2, 1), (3, 2, 2))
SPOT_OF_CLASS = (0, 6, 7, 2, 3, 1, 4, 5)


def pick(index, table):
    out = jnp.int32(table[0])
    for at, value in enumerate(table):
        if at:
            out = jnp.where(index == at, jnp.int32(value), out)
    return out


def pick_vec(index, table):
    out = jnp.full_like(index, table[0])
    for at, value in enumerate(table):
        if at:
            out = jnp.where(index == at, jnp.int32(value), out)
    return out


def device_of(g, c, u):
    spot = 4 * c + lax.div(u, 2)
    turn = lax.div(g, 2)
    x = lax.rem(pick(spot, [p[0] for p in PLACE]) + turn, 4)
    y = lax.rem(pick(spot, [p[1] for p in PLACE]) + turn, 4)
    z = lax.rem(pick(spot, [p[2] for p in PLACE]) + 2 * lax.rem(g, 2), 4)
    return 2 * x + lax.rem(u, 2), 4 * z + y


def my_place():
    grp, mem = lax.axis_index("grp"), lax.axis_index("mem")
    x, core = lax.div(grp, 2), lax.rem(grp, 2)
    z, y = lax.div(mem, 4), lax.rem(mem, 4)
    spot = pick(2 * lax.rem(x - y + 4, 4) + lax.rem(z, 2), SPOT_OF_CLASS)
    turn = lax.rem(x - pick(spot, [p[0] for p in PLACE]) + 4, 4)
    g = 2 * turn + lax.div(lax.rem(z - pick(spot, [p[2] for p in PLACE]) + 4, 4), 2)
    return grp, mem, g, lax.div(spot, 4), 2 * lax.rem(spot, 4) + core, core


FLAT_SHARERS = [k for row in SHARERS for k in row]
FLAT_POS = [BLOCKS[k].index(b) for b in range(4) for k in SHARERS[b]]
FLAT_BLOCKS = [b for pair in BLOCKS for b in pair]
FLAT_TURN = [SHARERS[BLOCKS[k][p]].index(k) for k in range(8) for p in range(2)]

FLOW = 6

NT = (((1,), (1,)), ((), ()))
NN = (((1,), (0,)), ((), ()))


def mm(a, b, dims=NN):
    return lax.dot_general(a, b, dims, preferred_element_type=F32)


def goes(block, t, turn):
    return (lax.rem(turn, 2) == t % 2) | ((block < 2) & (t >= 2))


def kernel(emb_ref, clu_ref, rank_ref, out_ref, unit, packed, arrived, split, held, acc, pbest,
           rbest, rep, back, bias, send0, recv0, send1, recv1, send2, recv2, send3, recv3, send4):
    grp, mem, g, mine_c, k, core = my_place()
    me = grp * 16 + mem

    barrier = pltpu.get_barrier_semaphore()

    @pl.loop(1, DEVS)
    def _(j):
        d = lax.rem(me + j, DEVS)
        pl.semaphore_signal(barrier, inc=1, device_id=(lax.div(d, 16), lax.rem(d, 16)), device_id_type=MESH)

    @pl.loop(0, 4)
    def _(i):
        rows = pl.ds(pl.multiple_of(i * 256, 256), 256)
        wide = emb_ref[rows, :].astype(F32)
        total = jnp.sum(wide * wide, axis=1, keepdims=True)
        unit[rows, :] = (wide * lax.rsqrt(total + 1e-06)).astype(BF)

    clu, rank = clu_ref[...], rank_ref[...]
    alive = clu >= 0
    vg = clu >> 1
    vh = rank >> 8
    share = ((vh >> 3) << 2) + ((vh & 7) >> 1)
    vk = pick_vec(share, FLAT_SHARERS)
    vp = pick_vec(share, FLAT_POS)
    vs = 4 * (vh & 1) + (vk >> 1)
    vx = (pick_vec(vs, [p[0] for p in PLACE]) + (vg >> 1)) & 3
    vy = (pick_vec(vs, [p[1] for p in PLACE]) + (vg >> 1)) & 3
    vz = (pick_vec(vs, [p[2] for p in PLACE]) + 2 * (vg & 1)) & 3
    vdev = (2 * vx + (vk & 1)) * 16 + 4 * vz + vy
    bucket = jnp.where(alive, 2 * vdev + vp, -1)
    low = lax.broadcasted_iota(I32, (128, 256), 0)
    col = lax.broadcasted_iota(I32, (128, 256), 1)
    tri = jnp.where((low < col) | (col >= 128), 1.0, 0.0).astype(BF)
    carry = jnp.zeros((256, 128), F32)
    bid = lax.broadcasted_iota(I32, (256, 128), 0)
    spots = []
    for i in range(8):
        hit = bid == bucket[:, i * 128 : (i + 1) * 128]
        counts = mm(jnp.where(hit, 1.0, 0.0).astype(BF), tri)
        spots.append(jnp.sum(jnp.where(hit, counts[:, :128] + carry, 0.0), axis=0, keepdims=True))
        carry = carry + counts[:, 128:]
    spot = jnp.concatenate(spots, axis=1).astype(I32)
    send_at = jnp.where(alive, bucket * 4 + spot, -1)

    kind = lax.broadcasted_iota(I32, (128, ROWS), 0)
    labels = jnp.where(
        kind == 0, (rank & 255).astype(F32), jnp.where(kind == 1, (clu & 1).astype(F32), jnp.where(kind == 2, 1.0, 0.0))
    ).astype(BF)

    @pl.loop(0, 4)
    def _(i):
        line = lax.broadcasted_iota(I32, (256, ROWS), 0) + i * 256
        where_to = jnp.where(line == send_at, 1.0, 0.0).astype(BF)
        devs = pl.ds(pl.multiple_of(i * 32, 32), 32)
        packed[devs, :, 0:D] = mm(where_to, unit[...]).reshape(32, 8, D).astype(BF)
        packed[devs, :, D:WIDE] = mm(where_to, labels, NT).reshape(32, 8, 128).astype(BF)

    pl.semaphore_wait(barrier, DEVS - 1)

    pltpu.make_async_copy(packed.at[me], arrived.at[me], recv0).start()

    @pl.loop(1, DEVS)
    def _(j):
        d = lax.rem(me + 37 * j, DEVS)
        pltpu.make_async_remote_copy(
            src_ref=packed.at[d], dst_ref=arrived.at[me], send_sem=send0, recv_sem=recv0,
            device_id=(lax.div(d, 16), lax.rem(d, 16)), device_id_type=MESH,
        ).start()

    acc[...] = jnp.full(acc.shape, -1.0, F32)
    pltpu.make_async_copy(arrived, arrived, recv0).wait()

    got = arrived[...].reshape(ROWS, WIDE)
    got_labels = got[:, D:WIDE]
    lane = lax.broadcasted_iota(I32, (8, 128), 1)
    weigh = jnp.where(lane == 0, 1.0, jnp.where(lane == 1, 256.0, jnp.where(lane == 2, 2048.0, 0.0))).astype(BF)
    slot_row = mm(weigh, got_labels, NT)[0:1, :].astype(I32)
    arr_i = lax.broadcasted_iota(I32, (1, ROWS), 1)
    slot_row = jnp.where(slot_row >= 2048, slot_row - 2048 + ((arr_i >> 2) & 1) * 512, -1)
    first = lax.broadcasted_iota(I32, (256, 128), 1) == 0

    for b in range(2):
        block = pick(2 * k + b, FLAT_BLOCKS)
        turn = pick(2 * k + b, FLAT_TURN)
        for c in range(2):
            n = 2 * b + c
            line = lax.broadcasted_iota(I32, (256, ROWS), 0) + n * 256
            where_to = jnp.where(line == slot_row, 1.0, 0.0).astype(BF)
            rows = mm(where_to, got)
            here = rows[:, D + 2 : D + 3]
            split[n, :, 0:128] = jnp.where(first & (here < 0.5), 256.0, rows[:, 0:128]).astype(BF)
            split[n, :, 128:D] = rows[:, 128:D].astype(BF)
            for t in range(4):
                other = pick(4 * block + t, FLAT_SHARERS)
                pos = pick(4 * block + t, FLAT_POS)
                wanted = goes(block, t, turn)
                mine = (other == k) & (mine_c == c)
                slot = 2 * turn + mine_c

                @pl.when(mine)
                def _():
                    pltpu.make_async_copy(split.at[n], held.at[pos, slot], recv1.at[pos, slot]).start()

                @pl.when(wanted & jnp.logical_not(mine))
                def _():
                    pltpu.make_async_remote_copy(
                        src_ref=split.at[n], dst_ref=held.at[pos, slot], send_sem=send1.at[n, t],
                        recv_sem=recv1.at[pos, slot], device_id=device_of(g, c, other), device_id_type=MESH,
                    ).start()

    diagonal = (k == 1) | (k == 7)
    both = (k < 2) | (k >= 6)
    probe = jnp.where(lax.broadcasted_iota(I32, (8, D), 1) == 0, 1.0, 0.0).astype(BF)

    def passes(p, s):
        yes = lax.rem(lax.div(s, 2), 2) == core
        return yes if p else yes & both

    def arrive(s):
        for p in range(2):
            pltpu.make_async_copy(held.at[p, s], held.at[p, s], recv1.at[p, s]).wait()

            @pl.when(passes(p, s))
            def _():
                pltpu.make_async_remote_copy(
                    src_ref=held.at[p, s], dst_ref=held.at[p, s], send_sem=send4.at[p, s], recv_sem=recv1.at[p, s],
                    device_id=(grp + 1 - 2 * core, mem), device_id_type=MESH,
                ).start()

        for p in range(2):
            mark = mm(probe, held[p, s], NT)[0:1, :]
            bias[p, s] = jnp.where(mark > 2.0, -1e4, 0.0)

    def tile(pr, a, pc, b, below=None):
        sims = mm(held[pr, a], held[pc, b], NT) + bias[pc, b]
        if below is not None:
            sims = jnp.where(below, sims, -1.0)
        acc[pr, a] = jnp.maximum(acc[pr, a], jnp.maximum(sims[:, :128], sims[:, 128:]))

    @pl.loop(0, FLOW)
    def _(s):
        arrive(s)

        @pl.when(jnp.logical_not(diagonal))
        def _():
            @pl.loop(0, s + 1)
            def _(a):
                tile(1, a, 0, s)

            @pl.loop(0, s)
            def _(b):
                tile(1, s, 0, b)

        @pl.when(diagonal)
        def _():
            for p in range(2):
                @pl.loop(0, s)
                def _(b):
                    tile(p, s, p, b)

                tile(p, s, p, s, lax.broadcasted_iota(I32, (256, 256), 1) < lax.broadcasted_iota(I32, (256, 256), 0))

    for s in range(FLOW, 8):
        arrive(s)

        @pl.when(jnp.logical_not(diagonal))
        def _():
            sims = mm(held[1, 0 : s + 1].reshape((s + 1) * 256, D), held[0, s], NT) + bias[0, s]
            sims = jnp.maximum(sims[:, :128], sims[:, 128:]).reshape(s + 1, 256, 128)
            acc[1, 0 : s + 1] = jnp.maximum(acc[1, 0 : s + 1], sims)
            sims = mm(held[1, s], held[0, 0:s].reshape(s * 256, D), NT)
            top = acc[1, s]
            for b in range(s):
                one = sims[:, b * 256 : (b + 1) * 256] + bias[0, b]
                top = jnp.maximum(top, jnp.maximum(one[:, :128], one[:, 128:]))
            acc[1, s] = top

        @pl.when(diagonal)
        def _():
            @pl.loop(0, 2)
            def _(p):
                sims = mm(held[p, s], held[p, 0 : s + 1].reshape((s + 1) * 256, D), NT)
                top = acc[p, s]
                for b in range(s + 1):
                    one = sims[:, b * 256 : (b + 1) * 256] + bias[p, b]
                    if b == s:
                        below = lax.broadcasted_iota(I32, (256, 256), 1) < lax.broadcasted_iota(I32, (256, 256), 0)
                        one = jnp.where(below, one, -1.0)
                    top = jnp.maximum(top, jnp.maximum(one[:, :128], one[:, 128:]))
                acc[p, s] = top

    for p in range(2):
        block = pick(2 * k + p, FLAT_BLOCKS)
        turn = pick(2 * k + p, FLAT_TURN)

        @pl.loop(0, 8)
        def _(a):
            pbest[p, a] = jnp.max(acc[p, a].T, axis=0, keepdims=True)

        for t in range(4):
            other = pick(4 * block + t, FLAT_SHARERS)
            pos = pick(4 * block + t, FLAT_POS)
            for c in range(2):
                mine = (other == k) & (mine_c == c)
                to = rbest.at[pos, mine_c, turn]
                sem = recv2.at[pos, mine_c, turn]

                @pl.when(mine)
                def _():
                    pltpu.make_async_copy(pbest.at[p, 2 * t + c], to, sem).start()

                @pl.when(jnp.logical_not(mine))
                def _():
                    pltpu.make_async_remote_copy(
                        src_ref=pbest.at[p, 2 * t + c], dst_ref=to, send_sem=send2.at[p, t, c],
                        recv_sem=sem, device_id=device_of(g, c, other), device_id_type=MESH,
                    ).start()

    wi = lax.broadcasted_iota(I32, (128, 128), 0)
    weights = jnp.where(wi == 0, 1.0, jnp.where(wi == 1, 256.0, jnp.where(wi == 2, 2048.0, 0.0))).astype(BF)
    slot_all = mm(arrived[...].reshape(ROWS, WIDE)[:, D:WIDE], weights).astype(I32)
    sub = lax.broadcasted_iota(I32, (ROWS, 128), 0) & 7
    lanes = lax.broadcasted_iota(I32, (ROWS, 128), 1)
    slot_all = jnp.where(slot_all >= 2048, slot_all - 2048 + (sub >> 2) * 512, -1)

    @pl.loop(0, 16)
    def _(i):
        p, c, t = lax.div(i, 8), lax.rem(lax.div(i, 4), 2), lax.rem(i, 4)
        pltpu.make_async_copy(rbest.at[p, c, t], rbest.at[p, c, t], recv2.at[p, c, t]).wait()

    value = jnp.full((ROWS, 128), -1.0, F32)
    for b in range(2):
        for c in range(2):
            best = jnp.maximum(
                jnp.maximum(rbest[b, c, 0], rbest[b, c, 1]), jnp.maximum(rbest[b, c, 2], rbest[b, c, 3])
            )
            for e in range(2):
                at = lanes + (b * 512 + c * 256 + e * 128)
                value = jnp.where(slot_all == at, best[:, e * 128 : (e + 1) * 128], value)
    value = jnp.max(value, axis=1, keepdims=True)
    value = jnp.where(lanes == sub, value, -1.0).reshape(DEVS, 8, 128)
    rep[...] = jnp.max(value, axis=1, keepdims=True)

    pltpu.make_async_copy(rep.at[me], back.at[me], recv3).start()

    @pl.loop(1, DEVS)
    def _(j):
        d = lax.rem(me + 37 * j, DEVS)
        pltpu.make_async_remote_copy(
            src_ref=rep.at[d], dst_ref=back.at[me], send_sem=send3, recv_sem=recv3,
            device_id=(lax.div(d, 16), lax.rem(d, 16)), device_id_type=MESH,
        ).start()

    pltpu.make_async_copy(back, back, recv3).wait()
    mine = jnp.broadcast_to(back[...], (DEVS, 8, 128)).reshape(ROWS, 128)
    mine = jnp.max(jnp.where(lanes == sub, mine, -1.0), axis=1, keepdims=True)
    line = lax.broadcasted_iota(I32, (ROWS, 128), 0)
    for i in range(8):
        part = slice(i * 128, (i + 1) * 128)
        out_ref[:, part] = jnp.max(jnp.where(line == send_at[:, part], mine, -1.0), axis=0, keepdims=True)

    some = packed.at[pl.ds(0, DEVS - 1)]
    pltpu.make_async_copy(some, some, send0).wait()
    some = rep.at[pl.ds(0, DEVS - 1)]
    pltpu.make_async_copy(some, some, send3).wait()
    for b in range(2):
        block = pick(2 * k + b, FLAT_BLOCKS)
        turn = pick(2 * k + b, FLAT_TURN)
        for t in range(4):
            other = pick(4 * block + t, FLAT_SHARERS)
            for c in range(2):
                away = jnp.logical_not((other == k) & (mine_c == c))

                @pl.when(away & goes(block, t, turn))
                def _():
                    pltpu.make_async_copy(split.at[2 * b + c], split.at[2 * b + c], send1.at[2 * b + c, t]).wait()

                @pl.when(away)
                def _():
                    pltpu.make_async_copy(pbest.at[b, 2 * t + c], pbest.at[b, 2 * t + c], send2.at[b, t, c]).wait()

        @pl.loop(0, 8)
        def _(s):
            @pl.when(passes(b, s))
            def _():
                pltpu.make_async_copy(held.at[b, s], held.at[b, s], send4.at[b, s]).wait()


def on_device(embeddings, cluster, rank):
    vmem = pl.BlockSpec(memory_space=pltpu.VMEM)
    out = pl.pallas_call(
        kernel,
        out_shape=jax.ShapeDtypeStruct((1, ROWS), F32),
        in_specs=[vmem] * 3,
        out_specs=vmem,
        scratch_shapes=[
            pltpu.VMEM((ROWS, D), BF),
            pltpu.VMEM((DEVS, 8, WIDE), BF),
            pltpu.VMEM((DEVS, 8, WIDE), BF),
            pltpu.VMEM((4, HALF, D), BF),
            pltpu.VMEM((2, 8, HALF, D), BF),
            pltpu.VMEM((2, 8, HALF, 128), F32),
            pltpu.VMEM((2, 8, 1, HALF), F32),
            pltpu.VMEM((2, 2, 4, 1, HALF), F32),
            pltpu.VMEM((DEVS, 1, 128), F32),
            pltpu.VMEM((DEVS, 1, 128), F32),
            pltpu.VMEM((2, 8, 1, HALF), F32),
            pltpu.SemaphoreType.DMA,
            pltpu.SemaphoreType.DMA,
            pltpu.SemaphoreType.DMA((4, 4)),
            pltpu.SemaphoreType.DMA((2, 8)),
            pltpu.SemaphoreType.DMA((2, 4, 2)),
            pltpu.SemaphoreType.DMA((2, 2, 4)),
            pltpu.SemaphoreType.DMA,
            pltpu.SemaphoreType.DMA,
            pltpu.SemaphoreType.DMA((2, 8)),
        ],
        compiler_params=pltpu.CompilerParams(
            collective_id=0, has_side_effects=True, vmem_limit_bytes=56 * 2**20
        ),
        cost_estimate=pl.CostEstimate(flops=12_000_000_000, bytes_accessed=2_000_000, transcendentals=1024),
    )(embeddings, cluster.reshape(1, -1), rank.reshape(1, -1))
    return out.reshape(-1)


def solution(mesh):
    in_specs = (P(("grp", "mem"), None), P(("grp", "mem")), P(("grp", "mem")))
    out_specs = P(("grp", "mem"))
    return jax.shard_map(
        on_device, mesh=mesh, in_specs=in_specs, out_specs=out_specs, check_vma=False
    )
```

```python
import functools

import jax
import jax.numpy as jnp
from jax import lax
from jax.experimental import pallas as pl
from jax.experimental.pallas import tpu as pltpu
from jax.sharding import PartitionSpec as P

MESH = pl.DeviceIdType.MESH
D = 768
WIDE = 896
ROWS = 1024
HALF = 256
DEVS = 128
BF = jnp.bfloat16
F32 = jnp.float32
I32 = jnp.int32

BLOCKS = ((0, 1), (0, 1), (0, 2), (1, 2), (0, 3), (1, 3), (2, 3), (2, 3))
SHARERS = ((0, 1, 2, 4), (0, 1, 3, 5), (2, 3, 6, 7), (4, 5, 6, 7))
PLACE = ((1, 1, 0), (0, 2, 1), (2, 1, 1), (3, 1, 2), (1, 2, 0), (0, 1, 1), (2, 2, 1), (3, 2, 2))
SPOT_OF_CLASS = (0, 6, 7, 2, 3, 1, 4, 5)


def pick(index, table):
    out = jnp.int32(table[0])
    for at, value in enumerate(table):
        if at:
            out = jnp.where(index == at, jnp.int32(value), out)
    return out


def pick_vec(index, table):
    out = jnp.full_like(index, table[0])
    for at, value in enumerate(table):
        if at:
            out = jnp.where(index == at, jnp.int32(value), out)
    return out


def device_of(g, c, u):
    spot = 4 * c + lax.div(u, 2)
    turn = lax.div(g, 2)
    x = lax.rem(pick(spot, [p[0] for p in PLACE]) + turn, 4)
    y = lax.rem(pick(spot, [p[1] for p in PLACE]) + turn, 4)
    z = lax.rem(pick(spot, [p[2] for p in PLACE]) + 2 * lax.rem(g, 2), 4)
    return 2 * x + lax.rem(u, 2), 4 * z + y


def my_place():
    grp, mem = lax.axis_index("grp"), lax.axis_index("mem")
    x, core = lax.div(grp, 2), lax.rem(grp, 2)
    z, y = lax.div(mem, 4), lax.rem(mem, 4)
    spot = pick(2 * lax.rem(x - y + 4, 4) + lax.rem(z, 2), SPOT_OF_CLASS)
    turn = lax.rem(x - pick(spot, [p[0] for p in PLACE]) + 4, 4)
    g = 2 * turn + lax.div(lax.rem(z - pick(spot, [p[2] for p in PLACE]) + 4, 4), 2)
    return grp, mem, g, lax.div(spot, 4), 2 * lax.rem(spot, 4) + core, core


FLAT_SHARERS = [k for row in SHARERS for k in row]
FLAT_POS = [BLOCKS[k].index(b) for b in range(4) for k in SHARERS[b]]
FLAT_BLOCKS = [b for pair in BLOCKS for b in pair]
FLAT_TURN = [SHARERS[BLOCKS[k][p]].index(k) for k in range(8) for p in range(2)]

PIECES = 16
FLOW = 6

NT = (((1,), (1,)), ((), ()))
NN = (((1,), (0,)), ((), ()))


def mm(a, b, dims=NN):
    return lax.dot_general(a, b, dims, preferred_element_type=F32)


def goes(block, t, turn):
    return (lax.rem(turn, 2) == lax.rem(t, 2)) | ((block < 2) & (t >= 2))


def kernel(emb_ref, clu_ref, rank_ref, out_ref, unit, packed, arrived, split, held, acc, pbest,
           rbest, rep, back, bias, send0, recv0, send1, recv1, send2, recv2, send3, recv3, send4):
    grp, mem, g, mine_c, k, core = my_place()
    me = grp * 16 + mem

    barrier = pltpu.get_barrier_semaphore()

    @pl.loop(1, DEVS)
    def _(j):
        d = lax.rem(me + j, DEVS)
        pl.semaphore_signal(barrier, inc=1, device_id=(lax.div(d, 16), lax.rem(d, 16)), device_id_type=MESH)

    @pl.loop(0, 4)
    def _(i):
        rows = pl.ds(pl.multiple_of(i * 256, 256), 256)
        wide = emb_ref[rows, :].astype(F32)
        total = jnp.sum(wide * wide, axis=1, keepdims=True)
        unit[rows, :] = (wide * lax.rsqrt(total + 1e-06)).astype(BF)

    clu, rank = clu_ref[...], rank_ref[...]
    alive = clu >= 0
    vg = clu >> 1
    vh = rank >> 8
    share = ((vh >> 3) << 2) + ((vh & 7) >> 1)
    vk = pick_vec(share, FLAT_SHARERS)
    vp = pick_vec(share, FLAT_POS)
    vs = 4 * (vh & 1) + (vk >> 1)
    vx = (pick_vec(vs, [p[0] for p in PLACE]) + (vg >> 1)) & 3
    vy = (pick_vec(vs, [p[1] for p in PLACE]) + (vg >> 1)) & 3
    vz = (pick_vec(vs, [p[2] for p in PLACE]) + 2 * (vg & 1)) & 3
    vdev = (2 * vx + (vk & 1)) * 16 + 4 * vz + vy
    bucket = jnp.where(alive, 2 * vdev + vp, -1)
    low = lax.broadcasted_iota(I32, (128, 256), 0)
    col = lax.broadcasted_iota(I32, (128, 256), 1)
    tri = jnp.where((low < col) | (col >= 128), 1.0, 0.0).astype(BF)
    carry = jnp.zeros((256, 128), F32)
    bid = lax.broadcasted_iota(I32, (256, 128), 0)
    spots = []
    for i in range(8):
        hit = bid == bucket[:, i * 128 : (i + 1) * 128]
        counts = mm(jnp.where(hit, 1.0, 0.0).astype(BF), tri)
        spots.append(jnp.sum(jnp.where(hit, counts[:, :128] + carry, 0.0), axis=0, keepdims=True))
        carry = carry + counts[:, 128:]
    spot = jnp.concatenate(spots, axis=1).astype(I32)
    send_at = jnp.where(alive, bucket * 4 + spot, -1)

    kind = lax.broadcasted_iota(I32, (128, ROWS), 0)
    labels = jnp.where(
        kind == 0, (rank & 255).astype(F32), jnp.where(kind == 1, (clu & 1).astype(F32), jnp.where(kind == 2, 1.0, 0.0))
    ).astype(BF)

    @pl.loop(0, 4)
    def _(i):
        line = lax.broadcasted_iota(I32, (256, ROWS), 0) + i * 256
        where_to = jnp.where(line == send_at, 1.0, 0.0).astype(BF)
        devs = pl.ds(pl.multiple_of(i * 32, 32), 32)
        packed[devs, :, 0:D] = mm(where_to, unit[...]).reshape(32, 8, D).astype(BF)
        packed[devs, :, D:WIDE] = mm(where_to, labels, NT).reshape(32, 8, 128).astype(BF)

    pl.semaphore_wait(barrier, DEVS - 1)

    pltpu.make_async_copy(packed.at[me], arrived.at[me], recv0).start()

    @pl.loop(1, DEVS)
    def _(j):
        d = lax.rem(me + 37 * j, DEVS)
        pltpu.make_async_remote_copy(
            src_ref=packed.at[d], dst_ref=arrived.at[me], send_sem=send0, recv_sem=recv0,
            device_id=(lax.div(d, 16), lax.rem(d, 16)), device_id_type=MESH,
        ).start()

    acc[...] = jnp.full(acc.shape, -1.0, F32)
    pltpu.make_async_copy(arrived, arrived, recv0).wait()

    got = arrived[...].reshape(ROWS, WIDE)
    got_labels = got[:, D:WIDE]
    lane = lax.broadcasted_iota(I32, (8, 128), 1)
    weigh = jnp.where(lane == 0, 1.0, jnp.where(lane == 1, 256.0, jnp.where(lane == 2, 2048.0, 0.0))).astype(BF)
    slot_row = mm(weigh, got_labels, NT)[0:1, :].astype(I32)
    arr_i = lax.broadcasted_iota(I32, (1, ROWS), 1)
    slot_row = jnp.where(slot_row >= 2048, slot_row - 2048 + ((arr_i >> 2) & 1) * 512, -1)
    first = lax.broadcasted_iota(I32, (256, 128), 1) == 0

    for b in range(2):
        block = pick(2 * k + b, FLAT_BLOCKS)
        turn = pick(2 * k + b, FLAT_TURN)
        for c in range(2):
            n = 2 * b + c
            line = lax.broadcasted_iota(I32, (256, ROWS), 0) + n * 256
            where_to = jnp.where(line == slot_row, 1.0, 0.0).astype(BF)
            rows = mm(where_to, got)
            here = rows[:, D + 2 : D + 3]
            split[n, :, 0:128] = jnp.where(first & (here < 0.5), 256.0, rows[:, 0:128]).astype(BF)
            split[n, :, 128:D] = rows[:, 128:D].astype(BF)

    for b in range(2):
        turn = pick(2 * k + b, FLAT_TURN)
        slot = 2 * turn + mine_c
        pltpu.make_async_copy(split.at[2 * b + mine_c], held.at[b, slot], recv1.at[b, slot]).start()

    @pl.loop(0, PIECES)
    def _(piece):
        rows = pl.ds(pl.multiple_of(piece * (HALF // PIECES), HALF // PIECES), HALF // PIECES)
        for step in range(4):
            for b in range(2):
                block = pick(2 * k + b, FLAT_BLOCKS)
                turn = pick(2 * k + b, FLAT_TURN)
                t = lax.rem(turn + step, 4)
                other = pick(4 * block + t, FLAT_SHARERS)
                pos = pick(4 * block + t, FLAT_POS)
                slot = 2 * turn + mine_c
                for flip in range(2):
                    c = lax.rem(mine_c + flip, 2)

                    if step or flip:
                        @pl.when(goes(block, t, turn))
                        def _():
                            pltpu.make_async_remote_copy(
                                src_ref=split.at[2 * b + c, rows], dst_ref=held.at[pos, slot, rows],
                                send_sem=send1.at[2 * b + flip, step], recv_sem=recv1.at[pos, slot],
                                device_id=device_of(g, c, other), device_id_type=MESH,
                            ).start()

    diagonal = (k == 1) | (k == 7)
    both = (k < 2) | (k >= 6)
    probe = jnp.where(lax.broadcasted_iota(I32, (8, D), 1) == 0, 1.0, 0.0).astype(BF)

    def passes(p, s):
        yes = lax.rem(lax.div(s, 2), 2) == core
        return yes if p else yes & both

    def arrive(s):
        for p in range(2):
            pltpu.make_async_copy(held.at[p, s], held.at[p, s], recv1.at[p, s]).wait()

            @pl.when(passes(p, s))
            def _():
                pltpu.make_async_remote_copy(
                    src_ref=held.at[p, s], dst_ref=held.at[p, s], send_sem=send4.at[p, s], recv_sem=recv1.at[p, s],
                    device_id=(grp + 1 - 2 * core, mem), device_id_type=MESH,
                ).start()

        for p in range(2):
            mark = mm(probe, held[p, s], NT)[0:1, :]
            bias[p, s] = jnp.where(mark > 2.0, -1e4, 0.0)

    def tile(pr, a, pc, b, below=None):
        sims = mm(held[pr, a], held[pc, b], NT) + bias[pc, b]
        if below is not None:
            sims = jnp.where(below, sims, -1.0)
        acc[pr, a] = jnp.maximum(acc[pr, a], jnp.maximum(sims[:, :128], sims[:, 128:]))

    @pl.loop(0, FLOW)
    def _(s):
        arrive(s)

        @pl.when(jnp.logical_not(diagonal))
        def _():
            @pl.loop(0, s + 1)
            def _(a):
                tile(1, a, 0, s)

            @pl.loop(0, s)
            def _(b):
                tile(1, s, 0, b)

        @pl.when(diagonal)
        def _():
            for p in range(2):
                @pl.loop(0, s)
                def _(b):
                    tile(p, s, p, b)

                tile(p, s, p, s, lax.broadcasted_iota(I32, (256, 256), 1) < lax.broadcasted_iota(I32, (256, 256), 0))

    for s in range(FLOW, 8):
        arrive(s)

        @pl.when(jnp.logical_not(diagonal))
        def _():
            sims = mm(held[1, 0 : s + 1].reshape((s + 1) * 256, D), held[0, s], NT) + bias[0, s]
            sims = jnp.maximum(sims[:, :128], sims[:, 128:]).reshape(s + 1, 256, 128)
            acc[1, 0 : s + 1] = jnp.maximum(acc[1, 0 : s + 1], sims)
            sims = mm(held[1, s], held[0, 0:s].reshape(s * 256, D), NT)
            top = acc[1, s]
            for b in range(s):
                one = sims[:, b * 256 : (b + 1) * 256] + bias[0, b]
                top = jnp.maximum(top, jnp.maximum(one[:, :128], one[:, 128:]))
            acc[1, s] = top

        @pl.when(diagonal)
        def _():
            @pl.loop(0, 2)
            def _(p):
                sims = mm(held[p, s], held[p, 0 : s + 1].reshape((s + 1) * 256, D), NT)
                top = acc[p, s]
                for b in range(s + 1):
                    one = sims[:, b * 256 : (b + 1) * 256] + bias[p, b]
                    if b == s:
                        below = lax.broadcasted_iota(I32, (256, 256), 1) < lax.broadcasted_iota(I32, (256, 256), 0)
                        one = jnp.where(below, one, -1.0)
                    top = jnp.maximum(top, jnp.maximum(one[:, :128], one[:, 128:]))
                acc[p, s] = top

    for p in range(2):
        block = pick(2 * k + p, FLAT_BLOCKS)
        turn = pick(2 * k + p, FLAT_TURN)

        @pl.loop(0, 8)
        def _(a):
            pbest[p, a] = jnp.max(acc[p, a].T, axis=0, keepdims=True)

        for t in range(4):
            other = pick(4 * block + t, FLAT_SHARERS)
            pos = pick(4 * block + t, FLAT_POS)
            for c in range(2):
                mine = (other == k) & (mine_c == c)
                to = rbest.at[pos, mine_c, turn]
                sem = recv2.at[pos, mine_c, turn]

                @pl.when(mine)
                def _():
                    pltpu.make_async_copy(pbest.at[p, 2 * t + c], to, sem).start()

                @pl.when(jnp.logical_not(mine))
                def _():
                    pltpu.make_async_remote_copy(
                        src_ref=pbest.at[p, 2 * t + c], dst_ref=to, send_sem=send2.at[p, t, c],
                        recv_sem=sem, device_id=device_of(g, c, other), device_id_type=MESH,
                    ).start()

    wi = lax.broadcasted_iota(I32, (128, 128), 0)
    weights = jnp.where(wi == 0, 1.0, jnp.where(wi == 1, 256.0, jnp.where(wi == 2, 2048.0, 0.0))).astype(BF)
    slot_all = mm(arrived[...].reshape(ROWS, WIDE)[:, D:WIDE], weights).astype(I32)
    sub = lax.broadcasted_iota(I32, (ROWS, 128), 0) & 7
    lanes = lax.broadcasted_iota(I32, (ROWS, 128), 1)
    slot_all = jnp.where(slot_all >= 2048, slot_all - 2048 + (sub >> 2) * 512, -1)

    @pl.loop(0, 16)
    def _(i):
        p, c, t = lax.div(i, 8), lax.rem(lax.div(i, 4), 2), lax.rem(i, 4)
        pltpu.make_async_copy(rbest.at[p, c, t], rbest.at[p, c, t], recv2.at[p, c, t]).wait()

    value = jnp.full((ROWS, 128), -1.0, F32)
    for b in range(2):
        for c in range(2):
            best = jnp.maximum(
                jnp.maximum(rbest[b, c, 0], rbest[b, c, 1]), jnp.maximum(rbest[b, c, 2], rbest[b, c, 3])
            )
            for e in range(2):
                at = lanes + (b * 512 + c * 256 + e * 128)
                value = jnp.where(slot_all == at, best[:, e * 128 : (e + 1) * 128], value)
    value = jnp.max(value, axis=1, keepdims=True)
    value = jnp.where(lanes == sub, value, -1.0).reshape(DEVS, 8, 128)
    rep[...] = jnp.max(value, axis=1, keepdims=True)

    pltpu.make_async_copy(rep.at[me], back.at[me], recv3).start()

    @pl.loop(1, DEVS)
    def _(j):
        d = lax.rem(me + 37 * j, DEVS)
        pltpu.make_async_remote_copy(
            src_ref=rep.at[d], dst_ref=back.at[me], send_sem=send3, recv_sem=recv3,
            device_id=(lax.div(d, 16), lax.rem(d, 16)), device_id_type=MESH,
        ).start()

    pltpu.make_async_copy(back, back, recv3).wait()
    mine = jnp.broadcast_to(back[...], (DEVS, 8, 128)).reshape(ROWS, 128)
    mine = jnp.max(jnp.where(lanes == sub, mine, -1.0), axis=1, keepdims=True)
    line = lax.broadcasted_iota(I32, (ROWS, 128), 0)
    for i in range(8):
        part = slice(i * 128, (i + 1) * 128)
        out_ref[:, part] = jnp.max(jnp.where(line == send_at[:, part], mine, -1.0), axis=0, keepdims=True)

    some = packed.at[pl.ds(0, DEVS - 1)]
    pltpu.make_async_copy(some, some, send0).wait()
    some = rep.at[pl.ds(0, DEVS - 1)]
    pltpu.make_async_copy(some, some, send3).wait()
    for b in range(2):
        block = pick(2 * k + b, FLAT_BLOCKS)
        turn = pick(2 * k + b, FLAT_TURN)
        for step in range(4):
            for flip in range(2):
                if step or flip:
                    @pl.when(goes(block, lax.rem(turn + step, 4), turn))
                    def _():
                        pltpu.make_async_copy(split.at[0], split.at[0], send1.at[2 * b + flip, step]).wait()

        for t in range(4):
            other = pick(4 * block + t, FLAT_SHARERS)
            for c in range(2):
                @pl.when(jnp.logical_not((other == k) & (mine_c == c)))
                def _():
                    pltpu.make_async_copy(pbest.at[b, 2 * t + c], pbest.at[b, 2 * t + c], send2.at[b, t, c]).wait()

        @pl.loop(0, 8)
        def _(s):
            @pl.when(passes(b, s))
            def _():
                pltpu.make_async_copy(held.at[b, s], held.at[b, s], send4.at[b, s]).wait()


def on_device(embeddings, cluster, rank):
    vmem = pl.BlockSpec(memory_space=pltpu.VMEM)
    out = pl.pallas_call(
        kernel,
        out_shape=jax.ShapeDtypeStruct((1, ROWS), F32),
        in_specs=[vmem] * 3,
        out_specs=vmem,
        scratch_shapes=[
            pltpu.VMEM((ROWS, D), BF),
            pltpu.VMEM((DEVS, 8, WIDE), BF),
            pltpu.VMEM((DEVS, 8, WIDE), BF),
            pltpu.VMEM((4, HALF, D), BF),
            pltpu.VMEM((2, 8, HALF, D), BF),
            pltpu.VMEM((2, 8, HALF, 128), F32),
            pltpu.VMEM((2, 8, 1, HALF), F32),
            pltpu.VMEM((2, 2, 4, 1, HALF), F32),
            pltpu.VMEM((DEVS, 1, 128), F32),
            pltpu.VMEM((DEVS, 1, 128), F32),
            pltpu.VMEM((2, 8, 1, HALF), F32),
            pltpu.SemaphoreType.DMA,
            pltpu.SemaphoreType.DMA,
            pltpu.SemaphoreType.DMA((4, 4)),
            pltpu.SemaphoreType.DMA((2, 8)),
            pltpu.SemaphoreType.DMA((2, 4, 2)),
            pltpu.SemaphoreType.DMA((2, 2, 4)),
            pltpu.SemaphoreType.DMA,
            pltpu.SemaphoreType.DMA,
            pltpu.SemaphoreType.DMA((2, 8)),
        ],
        compiler_params=pltpu.CompilerParams(
            collective_id=0, has_side_effects=True, vmem_limit_bytes=56 * 2**20
        ),
        cost_estimate=pl.CostEstimate(flops=12_000_000_000, bytes_accessed=2_000_000, transcendentals=1024),
    )(embeddings, cluster.reshape(1, -1), rank.reshape(1, -1))
    return out.reshape(-1)


def solution(mesh):
    in_specs = (P(("grp", "mem"), None), P(("grp", "mem")), P(("grp", "mem")))
    out_specs = P(("grp", "mem"))
    return jax.shard_map(
        on_device, mesh=mesh, in_specs=in_specs, out_specs=out_specs, check_vma=False
    )
```

```python
import functools

import jax
import jax.numpy as jnp
from jax import lax
from jax.experimental import pallas as pl
from jax.experimental.pallas import tpu as pltpu
from jax.sharding import PartitionSpec as P

MESH = pl.DeviceIdType.MESH
D = 768
PART = 384
ROWS = 1024
HALF = 256
DEVS = 128
BF = jnp.bfloat16
F32 = jnp.float32
I32 = jnp.int32

BLOCKS = ((0, 1), (0, 1), (0, 2), (1, 2), (0, 3), (1, 3), (2, 3), (2, 3))
SHARERS = ((0, 2, 1, 4), (1, 3, 0, 5), (6, 7, 2, 3), (4, 5, 6, 7))
PLACE = ((1, 1, 0), (0, 2, 1), (2, 1, 1), (3, 1, 2), (1, 2, 0), (0, 1, 1), (2, 2, 1), (3, 2, 2))
SPOT_OF_CLASS = (0, 6, 7, 2, 3, 1, 4, 5)


def pick(index, table):
    out = jnp.int32(table[0])
    for at, value in enumerate(table):
        if at:
            out = jnp.where(index == at, jnp.int32(value), out)
    return out


def pick_vec(index, table):
    out = jnp.full_like(index, table[0])
    for at, value in enumerate(table):
        if at:
            out = jnp.where(index == at, jnp.int32(value), out)
    return out


def device_of(g, c, u):
    spot = 4 * c + lax.div(u, 2)
    turn = lax.div(g, 2)
    x = lax.rem(pick(spot, [p[0] for p in PLACE]) + turn, 4)
    y = lax.rem(pick(spot, [p[1] for p in PLACE]) + turn, 4)
    z = lax.rem(pick(spot, [p[2] for p in PLACE]) + 2 * lax.rem(g, 2), 4)
    return 2 * x + lax.rem(u, 2), 4 * z + y


def my_place():
    grp, mem = lax.axis_index("grp"), lax.axis_index("mem")
    x, core = lax.div(grp, 2), lax.rem(grp, 2)
    z, y = lax.div(mem, 4), lax.rem(mem, 4)
    spot = pick(2 * lax.rem(x - y + 4, 4) + lax.rem(z, 2), SPOT_OF_CLASS)
    turn = lax.rem(x - pick(spot, [p[0] for p in PLACE]) + 4, 4)
    g = 2 * turn + lax.div(lax.rem(z - pick(spot, [p[2] for p in PLACE]) + 4, 4), 2)
    return grp, mem, g, lax.div(spot, 4), 2 * lax.rem(spot, 4) + core, core


FLAT_SHARERS = [k for row in SHARERS for k in row]
FLAT_POS = [BLOCKS[k].index(b) for b in range(4) for k in SHARERS[b]]
FLAT_BLOCKS = [b for pair in BLOCKS for b in pair]
PHASE_POS = [p for k in range(8) for p in sorted((0, 1), key=lambda p: SHARERS[BLOCKS[k][p]].index(k))]
PHASE_BLOCK = [BLOCKS[k][PHASE_POS[2 * k + f]] for k in range(8) for f in range(2)]
PHASE_TURN = [SHARERS[PHASE_BLOCK[2 * k + f]].index(k) for k in range(8) for f in range(2)]
BLOCK_TURN = [SHARERS[BLOCKS[k][p]].index(k) for k in range(8) for p in range(2)]
FLAT_PHASE = [t // 2 for b in range(4) for t in range(4)]

PIECES = 16
NT = (((1,), (1,)), ((), ()))
NN = (((1,), (0,)), ((), ()))


def mm(a, b, dims=NN):
    return lax.dot_general(a, b, dims, preferred_element_type=F32)


def goes(block, other, core):
    return (lax.rem(other, 2) == core) | ((block < 2) & (other >= 2))


def kernel(emb_ref, clu_ref, rank_ref, out_ref, unit, packed, arrived, tag_out, tag_in, split, held, acc, pbest,
           rbest, rep, back, bias, send0, recv0, send1, recv1, send2, recv2, send3, recv3, send4, send5, recv5):
    grp, mem, g, mine_c, k, core = my_place()
    me = grp * 16 + mem
    rbest[...] = jnp.full(rbest.shape, -1.0, F32)

    barrier = pltpu.get_barrier_semaphore()

    @pl.loop(1, DEVS)
    def _(j):
        d = lax.rem(me + j, DEVS)
        pl.semaphore_signal(barrier, inc=1, device_id=(lax.div(d, 16), lax.rem(d, 16)), device_id_type=MESH)

    @pl.loop(0, 4)
    def _(i):
        rows = pl.ds(pl.multiple_of(i * 256, 256), 256)
        wide = emb_ref[rows, :].astype(F32)
        total = jnp.sum(wide * wide, axis=1, keepdims=True)
        unit[rows, :] = (wide * lax.rsqrt(total + 1e-06)).astype(BF)

    clu, rank = clu_ref[...], rank_ref[...]
    alive = clu >= 0
    vg = clu >> 1
    vh = rank >> 8
    share = ((vh >> 3) << 2) + ((vh & 7) >> 1)
    vk = pick_vec(share, FLAT_SHARERS)
    vp = pick_vec(share, FLAT_PHASE)
    vs = 4 * (vh & 1) + (vk >> 1)
    vx = (pick_vec(vs, [p[0] for p in PLACE]) + (vg >> 1)) & 3
    vy = (pick_vec(vs, [p[1] for p in PLACE]) + (vg >> 1)) & 3
    vz = (pick_vec(vs, [p[2] for p in PLACE]) + 2 * (vg & 1)) & 3
    vdev = (2 * vx + (vk & 1)) * 16 + 4 * vz + vy
    bucket = jnp.where(alive, 2 * vdev + vp, -1)
    low = lax.broadcasted_iota(I32, (128, 256), 0)
    col = lax.broadcasted_iota(I32, (128, 256), 1)
    tri = jnp.where((low < col) | (col >= 128), 1.0, 0.0).astype(BF)
    carry = jnp.zeros((256, 128), F32)
    bid = lax.broadcasted_iota(I32, (256, 128), 0)
    spots = []
    for i in range(8):
        hit = bid == bucket[:, i * 128 : (i + 1) * 128]
        counts = mm(jnp.where(hit, 1.0, 0.0).astype(BF), tri)
        spots.append(jnp.sum(jnp.where(hit, counts[:, :128] + carry, 0.0), axis=0, keepdims=True))
        carry = carry + counts[:, 128:]
    spot = jnp.concatenate(spots, axis=1).astype(I32)
    send_at = jnp.where(alive, bucket * 4 + spot, -1)

    kind = lax.broadcasted_iota(I32, (256, ROWS), 0)
    labels = jnp.where(kind < 128, (rank & 255).astype(F32), (clu & 1).astype(F32) + 2.0).astype(BF)
    own_lane = lax.broadcasted_iota(I32, (32, 8, 128), 2) == lax.broadcasted_iota(I32, (32, 8, 128), 1)

    @pl.loop(0, 4)
    def _(i):
        line = lax.broadcasted_iota(I32, (256, ROWS), 0) + i * 256
        where_to = jnp.where(line == send_at, 1.0, 0.0).astype(BF)
        code = mm(where_to, labels, NT)
        code = (code[:, :128] + 256.0 * code[:, 128:]).reshape(32, 8, 128)
        devs = pl.ds(pl.multiple_of(i * 32, 32), 32)
        tag_out[devs] = jnp.sum(jnp.where(own_lane, code, 0.0), axis=1, keepdims=True)

    def pack(f):
        @pl.loop(0, 2)
        def _(i):
            at = lax.broadcasted_iota(I32, (512, ROWS), 0)
            line = ((at >> 3) + i * 64) * 8 + f * 4 + (at & 3)
            where_to = jnp.where(line == send_at, 1.0, 0.0).astype(BF)
            front = (lax.broadcasted_iota(I32, (512, PART), 0) & 7) < 4
            rows = jnp.where(front, mm(where_to, unit[:, 0:PART]), mm(where_to, unit[:, PART:D]))
            packed[f, pl.ds(pl.multiple_of(i * 64, 64), 64)] = rows.reshape(64, 8, PART).astype(BF)

    def ship(src, dst, d, ssem, rsem):
        pltpu.make_async_remote_copy(
            src_ref=src, dst_ref=dst, send_sem=ssem, recv_sem=rsem,
            device_id=(lax.div(d, 16), lax.rem(d, 16)), device_id_type=MESH,
        ).start()

    pack(0)
    pl.semaphore_wait(barrier, DEVS - 1)

    pltpu.make_async_copy(tag_out.at[me], tag_in.at[me], recv5).start()
    pltpu.make_async_copy(packed.at[0, me], arrived.at[0, me], recv0.at[0]).start()

    @pl.loop(1, DEVS)
    def _(j):
        d = lax.rem(me + 37 * j, DEVS)
        ship(tag_out.at[d], tag_in.at[me], d, send5, recv5)
        ship(packed.at[0, d], arrived.at[0, me], d, send0.at[0], recv0.at[0])

    pack(1)
    pltpu.make_async_copy(packed.at[1, me], arrived.at[1, me], recv0.at[1]).start()

    @pl.loop(1, DEVS)
    def _(j):
        d = lax.rem(me + 37 * j, DEVS)
        ship(packed.at[1, d], arrived.at[1, me], d, send0.at[1], recv0.at[1])

    acc[...] = jnp.full(acc.shape, -1.0, F32)
    sub8 = lax.broadcasted_iota(I32, (DEVS, 8, 128), 1)
    lane8 = lax.broadcasted_iota(I32, (DEVS, 8, 128), 2)
    pltpu.make_async_copy(tag_in, tag_in, recv5).wait()

    lane = lax.broadcasted_iota(I32, (8, 128), 1)
    weigh = jnp.where(lane == 0, 1.0, jnp.where(lane == 1, 256.0, 0.0)).astype(BF)
    at_half = (lax.broadcasted_iota(I32, (1, ROWS), 1) >> 2) & 1
    lanes = lax.broadcasted_iota(I32, (ROWS, 128), 1)

    def tags(f):
        wide = jnp.broadcast_to(tag_in[...], (DEVS, 8, 128))
        wide = jnp.where(lane8 == f * 4 + (sub8 & 3), wide, 0.0)
        code = jnp.max(wide, axis=2, keepdims=True).reshape(ROWS, 1).astype(I32)
        both = jnp.where(lanes == 0, code & 255, jnp.where(lanes == 1, code >> 8, 0)).astype(F32).astype(BF)
        return mm(weigh, both, NT)[0:1, :].astype(I32) - 512

    slot_rows = [tags(f) for f in range(2)]
    first = lax.broadcasted_iota(I32, (256, 128), 1) == 0

    for f in range(2):
        pltpu.make_async_copy(arrived.at[f], arrived.at[f], recv0.at[f]).wait()
        got = arrived[f].reshape(ROWS, PART)
        for c in range(2):
            line = lax.broadcasted_iota(I32, (256, ROWS), 0) + c * 256
            front = jnp.where(line == jnp.where(at_half == 0, slot_rows[f], -1), 1.0, 0.0)
            rear = jnp.where(line == jnp.where(at_half == 1, slot_rows[f], -1), 1.0, 0.0)
            here = jnp.sum(front, axis=1, keepdims=True)
            rows = mm(front.astype(BF), got)
            split[2 * f + c, :, 0:128] = jnp.where(first & (here < 0.5), 256.0, rows[:, 0:128]).astype(BF)
            split[2 * f + c, :, 128:PART] = rows[:, 128:].astype(BF)
            split[2 * f + c, :, PART:D] = mm(rear.astype(BF), got).astype(BF)

        block = pick(2 * k + f, PHASE_BLOCK)
        turn = pick(2 * k + f, PHASE_TURN)
        slot = 2 * turn + mine_c
        to = held.at[pick(2 * k + f, PHASE_POS), slot]
        pltpu.make_async_copy(split.at[2 * f + mine_c], to, recv1.at[pick(2 * k + f, PHASE_POS), slot]).start()

        @pl.loop(0, PIECES)
        def _(piece):
            rows = pl.ds(pl.multiple_of(piece * (HALF // PIECES), HALF // PIECES), HALF // PIECES)
            for step in range(4):
                t = lax.rem(turn + step, 4)
                other = pick(4 * block + t, FLAT_SHARERS)
                pos = pick(4 * block + t, FLAT_POS)
                for flip in range(2):
                    c = lax.rem(mine_c + flip, 2)

                    if step or flip:
                        @pl.when(goes(block, other, core))
                        def _():
                            pltpu.make_async_remote_copy(
                                src_ref=split.at[2 * f + c, rows], dst_ref=held.at[pos, slot, rows],
                                send_sem=send1.at[2 * f + flip, step], recv_sem=recv1.at[pos, slot],
                                device_id=device_of(g, c, other), device_id_type=MESH,
                            ).start()

    diagonal = (k == 1) | (k == 7)
    both = (k < 2) | (k >= 6)
    probe = jnp.where(lax.broadcasted_iota(I32, (8, D), 1) == 0, 1.0, 0.0).astype(BF)

    def passes(p, s):
        owner = pick(4 * pick(2 * k + p, FLAT_BLOCKS) + lax.div(s, 2), FLAT_SHARERS)
        yes = lax.rem(owner, 2) == core
        return yes if p else yes & both

    def arrive(s):
        for p in range(2):
            pltpu.make_async_copy(held.at[p, s], held.at[p, s], recv1.at[p, s]).wait()

            @pl.when(passes(p, s))
            def _():
                pltpu.make_async_remote_copy(
                    src_ref=held.at[p, s], dst_ref=held.at[p, s], send_sem=send4.at[p, s], recv_sem=recv1.at[p, s],
                    device_id=(grp + 1 - 2 * core, mem), device_id_type=MESH,
                ).start()

        for p in range(2):
            mark = mm(probe, held[p, s], NT)[0:1, :]
            bias[p, s] = jnp.where(mark > 2.0, -1e4, 0.0)

    def compare(pr, lo, hi, pc, b, corner=False):
        n = hi - lo
        sims = mm(held[pr, lo:hi].reshape(n * 256, D), held[pc, b], NT) + bias[pc, b]
        if corner:
            below = lax.broadcasted_iota(I32, (n * 256, 256), 1) < lax.broadcasted_iota(I32, (n * 256, 256), 0)
            sims = jnp.where(below, sims, -1.0)
        sims = jnp.maximum(sims[:, :128], sims[:, 128:]).reshape(n, 256, 128)
        acc[pr, lo:hi] = jnp.maximum(acc[pr, lo:hi], sims)

    @pl.loop(0, 4)
    def _(s):
        arrive(s)

    @pl.when(jnp.logical_not(diagonal))
    def _():
        @pl.loop(0, 4)
        def _(b):
            compare(1, 0, 4, 0, b)

    @pl.when(diagonal)
    def _():
        @pl.loop(0, 2)
        def _(p):
            for b in range(4):
                compare(p, b, 4, p, b, True)

    @pl.loop(4, 8)
    def _(s):
        arrive(s)

    @pl.when(jnp.logical_not(diagonal))
    def _():
        @pl.loop(0, 4)
        def _(b):
            compare(1, 4, 8, 0, b)

        @pl.loop(4, 8)
        def _(b):
            compare(1, 0, 8, 0, b)

    @pl.when(diagonal)
    def _():
        @pl.loop(0, 2)
        def _(p):
            @pl.loop(0, 4)
            def _(b):
                compare(p, 4, 8, p, b)

            for b in range(4, 8):
                compare(p, b, 8, p, b, True)

    def partials(act):
        for p in range(2):
            block = pick(2 * k + p, FLAT_BLOCKS)
            turn = pick(2 * k + p, BLOCK_TURN)

            def go():
                for t in range(4):
                    other = pick(4 * block + t, FLAT_SHARERS)
                    pos = pick(4 * block + t, FLAT_POS)
                    for c in range(2):
                        act(p, 2 * t + c, other, c, rbest.at[pos, mine_c, turn], recv2.at[pos, mine_c, turn], send2.at[p, t, c])

            if p:
                go()
            else:
                pl.when(diagonal)(go)

    def leave(p, a, other, c, to, rsem, ssem):
        mine = (other == k) & (mine_c == c)

        @pl.when(mine)
        def _():
            pltpu.make_async_copy(pbest.at[p, a], to, rsem).start()

        @pl.when(jnp.logical_not(mine))
        def _():
            pltpu.make_async_remote_copy(
                src_ref=pbest.at[p, a], dst_ref=to, send_sem=ssem, recv_sem=rsem,
                device_id=device_of(g, c, other), device_id_type=MESH,
            ).start()

    def left(p, a, other, c, to, rsem, ssem):
        @pl.when(jnp.logical_not((other == k) & (mine_c == c)))
        def _():
            pltpu.make_async_copy(pbest.at[p, a], pbest.at[p, a], ssem).wait()

    def condense(p):
        for a in range(8):
            pbest[p, a] = jnp.max(acc[p, a].T, axis=0, keepdims=True)

    condense(1)

    @pl.when(diagonal)
    def _():
        condense(0)

    partials(leave)

    sub = lax.broadcasted_iota(I32, (ROWS, 128), 0) & 7
    code = jnp.where(lane8 == sub8, jnp.broadcast_to(tag_in[...], (DEVS, 8, 128)), 0.0)
    code = jnp.max(code, axis=2, keepdims=True).reshape(ROWS, 1).astype(I32)
    slot_all = jnp.where(code >= 512, code - 512 + (sub >> 2) * 512, -1)

    @pl.loop(0, 16)
    def _(i):
        p, c, t = lax.div(i, 8), lax.rem(lax.div(i, 4), 2), lax.rem(i, 4)
        at = 4 * pick(2 * k + p, FLAT_BLOCKS) + t
        other = pick(at, FLAT_SHARERS)

        @pl.when((pick(at, FLAT_POS) == 1) | (other == 1) | (other == 7))
        def _():
            pltpu.make_async_copy(rbest.at[p, c, t], rbest.at[p, c, t], recv2.at[p, c, t]).wait()

    value = jnp.full((ROWS, 128), -1.0, F32)
    flipped = pick(2 * k, PHASE_POS) == 1
    for f in range(2):
        for c in range(2):
            best = jnp.where(flipped, jnp.max(rbest[1 - f, c], axis=0), jnp.max(rbest[f, c], axis=0))
            for e in range(2):
                at = lanes + (f * 512 + c * 256 + e * 128)
                value = jnp.where(slot_all == at, best[:, e * 128 : (e + 1) * 128], value)
    value = jnp.max(value, axis=1, keepdims=True)
    value = jnp.where(lanes == sub, value, -1.0).reshape(DEVS, 8, 128)
    rep[...] = jnp.max(value, axis=1, keepdims=True)

    pltpu.make_async_copy(rep.at[me], back.at[me], recv3).start()

    @pl.loop(1, DEVS)
    def _(j):
        d = lax.rem(me + 37 * j, DEVS)
        pltpu.make_async_remote_copy(
            src_ref=rep.at[d], dst_ref=back.at[me], send_sem=send3, recv_sem=recv3,
            device_id=(lax.div(d, 16), lax.rem(d, 16)), device_id_type=MESH,
        ).start()

    pltpu.make_async_copy(back, back, recv3).wait()
    mine = jnp.broadcast_to(back[...], (DEVS, 8, 128)).reshape(ROWS, 128)
    mine = jnp.max(jnp.where(lanes == sub, mine, -1.0), axis=1, keepdims=True)
    line = lax.broadcasted_iota(I32, (ROWS, 128), 0)
    for i in range(8):
        part = slice(i * 128, (i + 1) * 128)
        out_ref[:, part] = jnp.max(jnp.where(line == send_at[:, part], mine, -1.0), axis=0, keepdims=True)

    some = tag_out.at[pl.ds(0, DEVS - 1)]
    pltpu.make_async_copy(some, some, send5).wait()
    some = rep.at[pl.ds(0, DEVS - 1)]
    pltpu.make_async_copy(some, some, send3).wait()
    for f in range(2):
        some = packed.at[f, pl.ds(0, DEVS - 1)]
        pltpu.make_async_copy(some, some, send0.at[f]).wait()
        block = pick(2 * k + f, PHASE_BLOCK)
        turn = pick(2 * k + f, PHASE_TURN)
        for step in range(4):
            for flip in range(2):
                if step or flip:
                    other = pick(4 * block + lax.rem(turn + step, 4), FLAT_SHARERS)

                    @pl.when(goes(block, other, core))
                    def _():
                        pltpu.make_async_copy(split.at[0], split.at[0], send1.at[2 * f + flip, step]).wait()

        @pl.loop(0, 8)
        def _(s):
            @pl.when(passes(f, s))
            def _():
                pltpu.make_async_copy(held.at[f, s], held.at[f, s], send4.at[f, s]).wait()

    partials(left)


def on_device(embeddings, cluster, rank):
    vmem = pl.BlockSpec(memory_space=pltpu.VMEM)
    out = pl.pallas_call(
        kernel,
        out_shape=jax.ShapeDtypeStruct((1, ROWS), F32),
        in_specs=[vmem] * 3,
        out_specs=vmem,
        scratch_shapes=[
            pltpu.VMEM((ROWS, D), BF),
            pltpu.VMEM((2, DEVS, 8, PART), BF),
            pltpu.VMEM((2, DEVS, 8, PART), BF),
            pltpu.VMEM((DEVS, 1, 128), F32),
            pltpu.VMEM((DEVS, 1, 128), F32),
            pltpu.VMEM((4, HALF, D), BF),
            pltpu.VMEM((2, 8, HALF, D), BF),
            pltpu.VMEM((2, 8, HALF, 128), F32),
            pltpu.VMEM((2, 8, 1, HALF), F32),
            pltpu.VMEM((2, 2, 4, 1, HALF), F32),
            pltpu.VMEM((DEVS, 1, 128), F32),
            pltpu.VMEM((DEVS, 1, 128), F32),
            pltpu.VMEM((2, 8, 1, HALF), F32),
            pltpu.SemaphoreType.DMA((2,)),
            pltpu.SemaphoreType.DMA((2,)),
            pltpu.SemaphoreType.DMA((4, 4)),
            pltpu.SemaphoreType.DMA((2, 8)),
            pltpu.SemaphoreType.DMA((2, 4, 2)),
            pltpu.SemaphoreType.DMA((2, 2, 4)),
            pltpu.SemaphoreType.DMA,
            pltpu.SemaphoreType.DMA,
            pltpu.SemaphoreType.DMA((2, 8)),
            pltpu.SemaphoreType.DMA,
            pltpu.SemaphoreType.DMA,
        ],
        compiler_params=pltpu.CompilerParams(
            collective_id=0, has_side_effects=True, vmem_limit_bytes=56 * 2**20
        ),
        cost_estimate=pl.CostEstimate(flops=12_000_000_000, bytes_accessed=2_000_000, transcendentals=1024),
    )(embeddings, cluster.reshape(1, -1), rank.reshape(1, -1))
    return out.reshape(-1)


def solution(mesh):
    in_specs = (P(("grp", "mem"), None), P(("grp", "mem")), P(("grp", "mem")))
    out_specs = P(("grp", "mem"))
    return jax.shard_map(
        on_device, mesh=mesh, in_specs=in_specs, out_specs=out_specs, check_vma=False
    )
```

```python
import functools

import jax
import jax.numpy as jnp
from jax import lax
from jax.experimental import pallas as pl
from jax.experimental.pallas import tpu as pltpu
from jax.sharding import PartitionSpec as P

MESH = pl.DeviceIdType.MESH
D = 768
PART = 384
ROWS = 1024
HALF = 256
DEVS = 128
BF = jnp.bfloat16
F32 = jnp.float32
I32 = jnp.int32

BLOCKS = ((0, 1), (0, 1), (0, 2), (1, 2), (0, 3), (1, 3), (2, 3), (2, 3))
SHARERS = ((0, 2, 1, 4), (1, 3, 0, 5), (6, 7, 2, 3), (4, 5, 6, 7))
PLACE = ((1, 3, 3), (1, 2, 2), (1, 2, 3), (0, 1, 3), (1, 3, 2), (0, 2, 2), (0, 2, 3), (0, 1, 2))
SHIFTS = ((0, 0, 2), (1, 3, 0), (2, 2, 0))


def chip_of(spot, g):
    return tuple((PLACE[spot][a] + sum((g >> i & 1) * SHIFTS[i][a] for i in range(3))) % 4 for a in range(3))


CHIPS = {chip_of(spot, g): 8 * spot + g for spot in range(8) for g in range(8)}
WHO = [CHIPS[x, y, z] for x in range(4) for y in range(4) for z in range(4)]


def pick(index, table):
    out = jnp.int32(table[0])
    for at, value in enumerate(table):
        if at:
            out = jnp.where(index == at, jnp.int32(value), out)
    return out


def pick_vec(index, table):
    out = jnp.full_like(index, table[0])
    for at, value in enumerate(table):
        if at:
            out = jnp.where(index == at, jnp.int32(value), out)
    return out


def device_of(g, c, u):
    spot = 4 * c + lax.div(u, 2)
    bits = (lax.rem(g, 2), lax.rem(lax.div(g, 2), 2), lax.div(g, 4))
    x, y, z = (
        lax.rem(pick(spot, [p[a] for p in PLACE]) + sum(bits[i] * SHIFTS[i][a] for i in range(3)), 4) for a in range(3)
    )
    return 2 * x + lax.rem(u, 2), 4 * z + y


def my_place():
    grp, mem = lax.axis_index("grp"), lax.axis_index("mem")
    x, core = lax.div(grp, 2), lax.rem(grp, 2)
    z, y = lax.div(mem, 4), lax.rem(mem, 4)
    who = pick(16 * x + 4 * y + z, WHO)
    spot, g = lax.div(who, 8), lax.rem(who, 8)
    return grp, mem, g, lax.div(spot, 4), 2 * lax.rem(spot, 4) + core, core


FLAT_SHARERS = [k for row in SHARERS for k in row]
FLAT_POS = [BLOCKS[k].index(b) for b in range(4) for k in SHARERS[b]]
FLAT_BLOCKS = [b for pair in BLOCKS for b in pair]
PHASE_POS = [p for k in range(8) for p in sorted((0, 1), key=lambda p: SHARERS[BLOCKS[k][p]].index(k))]
PHASE_BLOCK = [BLOCKS[k][PHASE_POS[2 * k + f]] for k in range(8) for f in range(2)]
PHASE_TURN = [SHARERS[PHASE_BLOCK[2 * k + f]].index(k) for k in range(8) for f in range(2)]
BLOCK_TURN = [SHARERS[BLOCKS[k][p]].index(k) for k in range(8) for p in range(2)]
FLAT_PHASE = [t // 2 for b in range(4) for t in range(4)]

PIECES = 16
NT = (((1,), (1,)), ((), ()))
NN = (((1,), (0,)), ((), ()))


def mm(a, b, dims=NN):
    return lax.dot_general(a, b, dims, preferred_element_type=F32)


def goes(block, other, core):
    return (lax.rem(other, 2) == core) | ((block < 2) & (other >= 2))


def kernel(emb_ref, clu_ref, rank_ref, out_ref, unit, packed, arrived, tag_out, tag_in, split, held, acc, pbest,
           rbest, rep, back, bias, send0, recv0, send1, recv1, send2, recv2, send3, recv3, send4, send5, recv5):
    grp, mem, g, mine_c, k, core = my_place()
    me = grp * 16 + mem
    rbest[...] = jnp.full(rbest.shape, -1.0, F32)

    barrier = pltpu.get_barrier_semaphore()

    @pl.loop(1, DEVS)
    def _(j):
        d = lax.rem(me + j, DEVS)
        pl.semaphore_signal(barrier, inc=1, device_id=(lax.div(d, 16), lax.rem(d, 16)), device_id_type=MESH)

    @pl.loop(0, 4)
    def _(i):
        rows = pl.ds(pl.multiple_of(i * 256, 256), 256)
        wide = emb_ref[rows, :].astype(F32)
        total = jnp.sum(wide * wide, axis=1, keepdims=True)
        unit[rows, :] = (wide * lax.rsqrt(total + 1e-06)).astype(BF)

    clu, rank = clu_ref[...], rank_ref[...]
    alive = clu >= 0
    vg = clu >> 1
    vh = rank >> 8
    share = ((vh >> 3) << 2) + ((vh & 7) >> 1)
    vk = pick_vec(share, FLAT_SHARERS)
    vp = pick_vec(share, FLAT_PHASE)
    vs = 4 * (vh & 1) + (vk >> 1)
    vx, vy, vz = (
        (pick_vec(vs, [p[a] for p in PLACE]) + sum((vg >> i & 1) * SHIFTS[i][a] for i in range(3))) & 3 for a in range(3)
    )
    vdev = (2 * vx + (vk & 1)) * 16 + 4 * vz + vy
    bucket = jnp.where(alive, 2 * vdev + vp, -1)
    low = lax.broadcasted_iota(I32, (128, 256), 0)
    col = lax.broadcasted_iota(I32, (128, 256), 1)
    tri = jnp.where((low < col) | (col >= 128), 1.0, 0.0).astype(BF)
    carry = jnp.zeros((256, 128), F32)
    bid = lax.broadcasted_iota(I32, (256, 128), 0)
    spots = []
    for i in range(8):
        hit = bid == bucket[:, i * 128 : (i + 1) * 128]
        counts = mm(jnp.where(hit, 1.0, 0.0).astype(BF), tri)
        spots.append(jnp.sum(jnp.where(hit, counts[:, :128] + carry, 0.0), axis=0, keepdims=True))
        carry = carry + counts[:, 128:]
    spot = jnp.concatenate(spots, axis=1).astype(I32)
    send_at = jnp.where(alive, bucket * 4 + spot, -1)

    kind = lax.broadcasted_iota(I32, (256, ROWS), 0)
    labels = jnp.where(kind < 128, (rank & 255).astype(F32), (clu & 1).astype(F32) + 2.0).astype(BF)
    own_lane = lax.broadcasted_iota(I32, (32, 8, 128), 2) == lax.broadcasted_iota(I32, (32, 8, 128), 1)

    @pl.loop(0, 4)
    def _(i):
        line = lax.broadcasted_iota(I32, (256, ROWS), 0) + i * 256
        where_to = jnp.where(line == send_at, 1.0, 0.0).astype(BF)
        code = mm(where_to, labels, NT)
        code = (code[:, :128] + 256.0 * code[:, 128:]).reshape(32, 8, 128)
        devs = pl.ds(pl.multiple_of(i * 32, 32), 32)
        tag_out[devs] = jnp.sum(jnp.where(own_lane, code, 0.0), axis=1, keepdims=True)

    def pack(f):
        @pl.loop(0, 2)
        def _(i):
            at = lax.broadcasted_iota(I32, (512, ROWS), 0)
            line = ((at >> 3) + i * 64) * 8 + f * 4 + (at & 3)
            where_to = jnp.where(line == send_at, 1.0, 0.0).astype(BF)
            front = (lax.broadcasted_iota(I32, (512, PART), 0) & 7) < 4
            rows = jnp.where(front, mm(where_to, unit[:, 0:PART]), mm(where_to, unit[:, PART:D]))
            packed[f, pl.ds(pl.multiple_of(i * 64, 64), 64)] = rows.reshape(64, 8, PART).astype(BF)

    def ship(src, dst, d, ssem, rsem):
        pltpu.make_async_remote_copy(
            src_ref=src, dst_ref=dst, send_sem=ssem, recv_sem=rsem,
            device_id=(lax.div(d, 16), lax.rem(d, 16)), device_id_type=MESH,
        ).start()

    pack(0)
    pl.semaphore_wait(barrier, DEVS - 1)

    pltpu.make_async_copy(tag_out.at[me], tag_in.at[me], recv5).start()
    pltpu.make_async_copy(packed.at[0, me], arrived.at[0, me], recv0.at[0]).start()

    @pl.loop(1, DEVS)
    def _(j):
        d = lax.rem(me + 37 * j, DEVS)
        ship(tag_out.at[d], tag_in.at[me], d, send5, recv5)
        ship(packed.at[0, d], arrived.at[0, me], d, send0.at[0], recv0.at[0])

    pack(1)
    pltpu.make_async_copy(packed.at[1, me], arrived.at[1, me], recv0.at[1]).start()

    @pl.loop(1, DEVS)
    def _(j):
        d = lax.rem(me + 37 * j, DEVS)
        ship(packed.at[1, d], arrived.at[1, me], d, send0.at[1], recv0.at[1])

    plan = []
    for p in range(2):
        block = pick(2 * k + p, FLAT_BLOCKS)
        turn = pick(2 * k + p, BLOCK_TURN)
        for a in range(8):
            other, c = pick(4 * block + a // 2, FLAT_SHARERS), a % 2
            pos = pick(4 * block + a // 2, FLAT_POS)
            plan.append((p, a, (other == k) & (mine_c == c), device_of(g, c, other), pos, turn))

    acc[...] = jnp.full(acc.shape, -1.0, F32)
    sub8 = lax.broadcasted_iota(I32, (DEVS, 8, 128), 1)
    lane8 = lax.broadcasted_iota(I32, (DEVS, 8, 128), 2)
    pltpu.make_async_copy(tag_in, tag_in, recv5).wait()

    lane = lax.broadcasted_iota(I32, (8, 128), 1)
    weigh = jnp.where(lane == 0, 1.0, jnp.where(lane == 1, 256.0, 0.0)).astype(BF)
    at_half = (lax.broadcasted_iota(I32, (1, ROWS), 1) >> 2) & 1
    lanes = lax.broadcasted_iota(I32, (ROWS, 128), 1)

    def tags(f):
        wide = jnp.broadcast_to(tag_in[...], (DEVS, 8, 128))
        wide = jnp.where(lane8 == f * 4 + (sub8 & 3), wide, 0.0)
        code = jnp.max(wide, axis=2, keepdims=True).reshape(ROWS, 1).astype(I32)
        both = jnp.where(lanes == 0, code & 255, jnp.where(lanes == 1, code >> 8, 0)).astype(F32).astype(BF)
        return mm(weigh, both, NT)[0:1, :].astype(I32) - 512

    slot_rows = [tags(f) for f in range(2)]
    first = lax.broadcasted_iota(I32, (256, 128), 1) == 0

    for f in range(2):
        pltpu.make_async_copy(arrived.at[f], arrived.at[f], recv0.at[f]).wait()
        got = arrived[f].reshape(ROWS, PART)
        for c in range(2):
            line = lax.broadcasted_iota(I32, (256, ROWS), 0) + c * 256
            front = jnp.where(line == jnp.where(at_half == 0, slot_rows[f], -1), 1.0, 0.0)
            rear = jnp.where(line == jnp.where(at_half == 1, slot_rows[f], -1), 1.0, 0.0)
            here = jnp.sum(front, axis=1, keepdims=True)
            rows = mm(front.astype(BF), got)
            split[2 * f + c, :, 0:128] = jnp.where(first & (here < 0.5), 256.0, rows[:, 0:128]).astype(BF)
            split[2 * f + c, :, 128:PART] = rows[:, 128:].astype(BF)
            split[2 * f + c, :, PART:D] = mm(rear.astype(BF), got).astype(BF)

        block = pick(2 * k + f, PHASE_BLOCK)
        turn = pick(2 * k + f, PHASE_TURN)
        slot = 2 * turn + mine_c
        to = held.at[pick(2 * k + f, PHASE_POS), slot]
        pltpu.make_async_copy(split.at[2 * f + mine_c], to, recv1.at[pick(2 * k + f, PHASE_POS), slot]).start()

        routes = []
        for step in range(4):
            t = lax.rem(turn + step, 4)
            other = pick(4 * block + t, FLAT_SHARERS)
            pos = pick(4 * block + t, FLAT_POS)
            for flip in range(2):
                if step or flip:
                    c = lax.rem(mine_c + flip, 2)
                    routes.append((step, flip, c, pos, goes(block, other, core), device_of(g, c, other)))

        @pl.loop(0, PIECES)
        def _(piece):
            rows = pl.ds(pl.multiple_of(piece * (HALF // PIECES), HALF // PIECES), HALF // PIECES)
            for step, flip, c, pos, wanted, device in routes:
                @pl.when(wanted)
                def _():
                    pltpu.make_async_remote_copy(
                        src_ref=split.at[2 * f + c, rows], dst_ref=held.at[pos, slot, rows],
                        send_sem=send1.at[2 * f + flip, step], recv_sem=recv1.at[pos, slot],
                        device_id=device, device_id_type=MESH,
                    ).start()

    diagonal = (k == 1) | (k == 7)
    both = (k < 2) | (k >= 6)
    probe = jnp.where(lax.broadcasted_iota(I32, (8, D), 1) == 0, 1.0, 0.0).astype(BF)

    def passes(p, s):
        owner = pick(4 * pick(2 * k + p, FLAT_BLOCKS) + lax.div(s, 2), FLAT_SHARERS)
        yes = lax.rem(owner, 2) == core
        return yes if p else yes & both

    def arrive(s):
        for p in range(2):
            pltpu.make_async_copy(held.at[p, s], held.at[p, s], recv1.at[p, s]).wait()

            @pl.when(passes(p, s))
            def _():
                pltpu.make_async_remote_copy(
                    src_ref=held.at[p, s], dst_ref=held.at[p, s], send_sem=send4.at[p, s], recv_sem=recv1.at[p, s],
                    device_id=(grp + 1 - 2 * core, mem), device_id_type=MESH,
                ).start()

        for p in range(2):
            mark = mm(probe, held[p, s], NT)[0:1, :]
            bias[p, s] = jnp.where(mark > 2.0, -1e4, 0.0)

    def compare(pr, lo, hi, pc, b, corner=False):
        n = hi - lo
        sims = mm(held[pr, lo:hi].reshape(n * 256, D), held[pc, b], NT) + bias[pc, b]
        if corner:
            below = lax.broadcasted_iota(I32, (n * 256, 256), 1) < lax.broadcasted_iota(I32, (n * 256, 256), 0)
            sims = jnp.where(below, sims, -1.0)
        sims = jnp.maximum(sims[:, :128], sims[:, 128:]).reshape(n, 256, 128)
        acc[pr, lo:hi] = jnp.maximum(acc[pr, lo:hi], sims)

    @pl.loop(0, 4)
    def _(s):
        arrive(s)

    @pl.when(jnp.logical_not(diagonal))
    def _():
        @pl.loop(0, 4)
        def _(b):
            compare(1, 0, 4, 0, b)

    @pl.when(diagonal)
    def _():
        @pl.loop(0, 2)
        def _(p):
            for b in range(4):
                compare(p, b, 4, p, b, True)

    @pl.loop(4, 8)
    def _(s):
        arrive(s)

    @pl.when(jnp.logical_not(diagonal))
    def _():
        @pl.loop(0, 4)
        def _(b):
            compare(1, 4, 8, 0, b)

        @pl.loop(4, 8)
        def _(b):
            compare(1, 0, 8, 0, b)

    @pl.when(diagonal)
    def _():
        @pl.loop(0, 2)
        def _(p):
            @pl.loop(0, 4)
            def _(b):
                compare(p, 4, 8, p, b)

            for b in range(4, 8):
                compare(p, b, 8, p, b, True)

    def leave(p):
        for _, a, mine, device, pos, turn in plan[8 * p : 8 * p + 8]:
            pbest[p, a] = jnp.max(acc[p, a].T, axis=0, keepdims=True)

            @pl.when(mine)
            def _():
                to = rbest.at[pos, mine_c, turn]
                pltpu.make_async_copy(pbest.at[p, a], to, recv2.at[pos, mine_c, turn]).start()

            @pl.when(jnp.logical_not(mine))
            def _():
                pltpu.make_async_remote_copy(
                    src_ref=pbest.at[p, a], dst_ref=rbest.at[pos, mine_c, turn], send_sem=send2.at[p, a // 2, a % 2],
                    recv_sem=recv2.at[pos, mine_c, turn], device_id=device, device_id_type=MESH,
                ).start()

    def left(p):
        for _, a, mine, device, pos, turn in plan[8 * p : 8 * p + 8]:
            @pl.when(jnp.logical_not(mine))
            def _():
                pltpu.make_async_copy(pbest.at[p, a], pbest.at[p, a], send2.at[p, a // 2, a % 2]).wait()

    leave(1)
    pl.when(diagonal)(lambda: leave(0))

    sub = lax.broadcasted_iota(I32, (ROWS, 128), 0) & 7
    code = jnp.where(lane8 == sub8, jnp.broadcast_to(tag_in[...], (DEVS, 8, 128)), 0.0)
    code = jnp.max(code, axis=2, keepdims=True).reshape(ROWS, 1).astype(I32)
    slot_all = jnp.where(code >= 512, code - 512 + (sub >> 2) * 512, -1)

    @pl.loop(0, 16)
    def _(i):
        p, c, t = lax.div(i, 8), lax.rem(lax.div(i, 4), 2), lax.rem(i, 4)
        at = 4 * pick(2 * k + p, FLAT_BLOCKS) + t
        other = pick(at, FLAT_SHARERS)

        @pl.when((pick(at, FLAT_POS) == 1) | (other == 1) | (other == 7))
        def _():
            pltpu.make_async_copy(rbest.at[p, c, t], rbest.at[p, c, t], recv2.at[p, c, t]).wait()

    value = jnp.full((ROWS, 128), -1.0, F32)
    flipped = pick(2 * k, PHASE_POS) == 1
    for f in range(2):
        for c in range(2):
            best = jnp.where(flipped, jnp.max(rbest[1 - f, c], axis=0), jnp.max(rbest[f, c], axis=0))
            for e in range(2):
                at = lanes + (f * 512 + c * 256 + e * 128)
                value = jnp.where(slot_all == at, best[:, e * 128 : (e + 1) * 128], value)
    value = jnp.max(value, axis=1, keepdims=True)
    value = jnp.where(lanes == sub, value, -1.0).reshape(DEVS, 8, 128)
    rep[...] = jnp.max(value, axis=1, keepdims=True)

    pltpu.make_async_copy(rep.at[me], back.at[me], recv3).start()

    @pl.loop(1, DEVS)
    def _(j):
        d = lax.rem(me + 37 * j, DEVS)
        pltpu.make_async_remote_copy(
            src_ref=rep.at[d], dst_ref=back.at[me], send_sem=send3, recv_sem=recv3,
            device_id=(lax.div(d, 16), lax.rem(d, 16)), device_id_type=MESH,
        ).start()

    pltpu.make_async_copy(back, back, recv3).wait()
    mine = jnp.broadcast_to(back[...], (DEVS, 8, 128)).reshape(ROWS, 128)
    mine = jnp.max(jnp.where(lanes == sub, mine, -1.0), axis=1, keepdims=True)
    line = lax.broadcasted_iota(I32, (ROWS, 128), 0)
    for i in range(8):
        part = slice(i * 128, (i + 1) * 128)
        out_ref[:, part] = jnp.max(jnp.where(line == send_at[:, part], mine, -1.0), axis=0, keepdims=True)

    some = tag_out.at[pl.ds(0, DEVS - 1)]
    pltpu.make_async_copy(some, some, send5).wait()
    some = rep.at[pl.ds(0, DEVS - 1)]
    pltpu.make_async_copy(some, some, send3).wait()
    for f in range(2):
        some = packed.at[f, pl.ds(0, DEVS - 1)]
        pltpu.make_async_copy(some, some, send0.at[f]).wait()
        block = pick(2 * k + f, PHASE_BLOCK)
        turn = pick(2 * k + f, PHASE_TURN)
        for step in range(4):
            for flip in range(2):
                if step or flip:
                    other = pick(4 * block + lax.rem(turn + step, 4), FLAT_SHARERS)

                    @pl.when(goes(block, other, core))
                    def _():
                        pltpu.make_async_copy(split.at[0], split.at[0], send1.at[2 * f + flip, step]).wait()

        @pl.loop(0, 8)
        def _(s):
            @pl.when(passes(f, s))
            def _():
                pltpu.make_async_copy(held.at[f, s], held.at[f, s], send4.at[f, s]).wait()

    left(1)
    pl.when(diagonal)(lambda: left(0))


def on_device(embeddings, cluster, rank):
    vmem = pl.BlockSpec(memory_space=pltpu.VMEM)
    out = pl.pallas_call(
        kernel,
        out_shape=jax.ShapeDtypeStruct((1, ROWS), F32),
        in_specs=[vmem] * 3,
        out_specs=vmem,
        scratch_shapes=[
            pltpu.VMEM((ROWS, D), BF),
            pltpu.VMEM((2, DEVS, 8, PART), BF),
            pltpu.VMEM((2, DEVS, 8, PART), BF),
            pltpu.VMEM((DEVS, 1, 128), F32),
            pltpu.VMEM((DEVS, 1, 128), F32),
            pltpu.VMEM((4, HALF, D), BF),
            pltpu.VMEM((2, 8, HALF, D), BF),
            pltpu.VMEM((2, 8, HALF, 128), F32),
            pltpu.VMEM((2, 8, 1, HALF), F32),
            pltpu.VMEM((2, 2, 4, 1, HALF), F32),
            pltpu.VMEM((DEVS, 1, 128), F32),
            pltpu.VMEM((DEVS, 1, 128), F32),
            pltpu.VMEM((2, 8, 1, HALF), F32),
            pltpu.SemaphoreType.DMA((2,)),
            pltpu.SemaphoreType.DMA((2,)),
            pltpu.SemaphoreType.DMA((4, 4)),
            pltpu.SemaphoreType.DMA((2, 8)),
            pltpu.SemaphoreType.DMA((2, 4, 2)),
            pltpu.SemaphoreType.DMA((2, 2, 4)),
            pltpu.SemaphoreType.DMA,
            pltpu.SemaphoreType.DMA,
            pltpu.SemaphoreType.DMA((2, 8)),
            pltpu.SemaphoreType.DMA,
            pltpu.SemaphoreType.DMA,
        ],
        compiler_params=pltpu.CompilerParams(
            collective_id=0, has_side_effects=True, vmem_limit_bytes=56 * 2**20
        ),
        cost_estimate=pl.CostEstimate(flops=12_000_000_000, bytes_accessed=2_000_000, transcendentals=1024),
    )(embeddings, cluster.reshape(1, -1), rank.reshape(1, -1))
    return out.reshape(-1)


def solution(mesh):
    in_specs = (P(("grp", "mem"), None), P(("grp", "mem")), P(("grp", "mem")))
    out_specs = P(("grp", "mem"))
    return jax.shard_map(
        on_device, mesh=mesh, in_specs=in_specs, out_specs=out_specs, check_vma=False
    )
```

```python
import functools

import jax
import jax.numpy as jnp
from jax import lax
from jax.experimental import pallas as pl
from jax.experimental.pallas import tpu as pltpu
from jax.sharding import PartitionSpec as P

MESH = pl.DeviceIdType.MESH
D = 768
PART = 384
ROWS = 1024
HALF = 256
DEVS = 128
BF = jnp.bfloat16
F32 = jnp.float32
I32 = jnp.int32

BLOCKS = ((0, 1), (0, 1), (0, 2), (1, 2), (0, 3), (1, 3), (2, 3), (2, 3))
SHARERS = ((0, 2, 1, 4), (1, 3, 0, 5), (6, 7, 2, 3), (4, 5, 6, 7))
PLACE = ((1, 3, 3), (1, 2, 2), (1, 2, 3), (0, 1, 3), (1, 3, 2), (0, 2, 2), (0, 2, 3), (0, 1, 2))
SHIFTS = ((0, 0, 2), (1, 3, 0), (2, 2, 0))


def chip_of(spot, g):
    return tuple((PLACE[spot][a] + sum((g >> i & 1) * SHIFTS[i][a] for i in range(3))) % 4 for a in range(3))


CHIPS = {chip_of(spot, g): 8 * spot + g for spot in range(8) for g in range(8)}
WHO = [CHIPS[x, y, z] for x in range(4) for y in range(4) for z in range(4)]


def pick(index, table):
    out = jnp.int32(table[0])
    for at, value in enumerate(table):
        if at:
            out = jnp.where(index == at, jnp.int32(value), out)
    return out


def pick_vec(index, table):
    out = jnp.full_like(index, table[0])
    for at, value in enumerate(table):
        if at:
            out = jnp.where(index == at, jnp.int32(value), out)
    return out


def device_of(g, c, u):
    spot = 4 * c + lax.div(u, 2)
    bits = (lax.rem(g, 2), lax.rem(lax.div(g, 2), 2), lax.div(g, 4))
    x, y, z = (
        lax.rem(pick(spot, [p[a] for p in PLACE]) + sum(bits[i] * SHIFTS[i][a] for i in range(3)), 4) for a in range(3)
    )
    return 2 * x + lax.rem(u, 2), 4 * z + y


def my_place():
    grp, mem = lax.axis_index("grp"), lax.axis_index("mem")
    x, core = lax.div(grp, 2), lax.rem(grp, 2)
    z, y = lax.div(mem, 4), lax.rem(mem, 4)
    who = pick(16 * x + 4 * y + z, WHO)
    spot, g = lax.div(who, 8), lax.rem(who, 8)
    return grp, mem, g, lax.div(spot, 4), 2 * lax.rem(spot, 4) + core, core


FLAT_SHARERS = [k for row in SHARERS for k in row]
FLAT_POS = [BLOCKS[k].index(b) for b in range(4) for k in SHARERS[b]]
FLAT_BLOCKS = [b for pair in BLOCKS for b in pair]
PHASE_POS = [p for k in range(8) for p in sorted((0, 1), key=lambda p: SHARERS[BLOCKS[k][p]].index(k))]
PHASE_BLOCK = [BLOCKS[k][PHASE_POS[2 * k + f]] for k in range(8) for f in range(2)]
PHASE_TURN = [SHARERS[PHASE_BLOCK[2 * k + f]].index(k) for k in range(8) for f in range(2)]
BLOCK_TURN = [SHARERS[BLOCKS[k][p]].index(k) for k in range(8) for p in range(2)]
FLAT_PHASE = [t // 2 for b in range(4) for t in range(4)]

PIECES = 16
NT = (((1,), (1,)), ((), ()))
NN = (((1,), (0,)), ((), ()))


def mm(a, b, dims=NN):
    return lax.dot_general(a, b, dims, preferred_element_type=F32)


def goes(block, other, core):
    return (lax.rem(other, 2) == core) | ((block < 2) & (other >= 2))


def kernel(emb_ref, clu_ref, rank_ref, out_ref, unit, packed, arrived, tag_out, tag_in, split, held, acc, pbest,
           rbest, rep, back, bias, send0, recv0, send1, recv1, send2, recv2, send3, recv3, send4, send5, recv5):
    grp, mem, g, mine_c, k, core = my_place()
    me = grp * 16 + mem
    rbest[...] = jnp.full(rbest.shape, -1.0, F32)

    barrier = pltpu.get_barrier_semaphore()

    @pl.loop(1, DEVS)
    def _(j):
        d = lax.rem(me + j, DEVS)
        pl.semaphore_signal(barrier, inc=1, device_id=(lax.div(d, 16), lax.rem(d, 16)), device_id_type=MESH)

    @pl.loop(0, 4)
    def _(i):
        rows = pl.ds(pl.multiple_of(i * 256, 256), 256)
        wide = emb_ref[rows, :].astype(F32)
        total = jnp.sum(wide * wide, axis=1, keepdims=True)
        unit[rows, :] = (wide * lax.rsqrt(total + 1e-06)).astype(BF)

    clu, rank = clu_ref[...], rank_ref[...]
    alive = clu >= 0
    vg = clu >> 1
    vh = rank >> 8
    share = ((vh >> 3) << 2) + ((vh & 7) >> 1)
    vk = pick_vec(share, FLAT_SHARERS)
    vp = pick_vec(share, FLAT_PHASE)
    vs = 4 * (vh & 1) + (vk >> 1)
    vx, vy, vz = (
        (pick_vec(vs, [p[a] for p in PLACE]) + sum((vg >> i & 1) * SHIFTS[i][a] for i in range(3))) & 3 for a in range(3)
    )
    vdev = (2 * vx + (vk & 1)) * 16 + 4 * vz + vy
    bucket = jnp.where(alive, 2 * vdev + vp, -1)
    low = lax.broadcasted_iota(I32, (128, 256), 0)
    col = lax.broadcasted_iota(I32, (128, 256), 1)
    tri = jnp.where((low < col) | (col >= 128), 1.0, 0.0).astype(BF)
    carry = jnp.zeros((256, 128), F32)
    bid = lax.broadcasted_iota(I32, (256, 128), 0)
    spots = []
    for i in range(8):
        hit = bid == bucket[:, i * 128 : (i + 1) * 128]
        counts = mm(jnp.where(hit, 1.0, 0.0).astype(BF), tri)
        spots.append(jnp.sum(jnp.where(hit, counts[:, :128] + carry, 0.0), axis=0, keepdims=True))
        carry = carry + counts[:, 128:]
    spot = jnp.concatenate(spots, axis=1).astype(I32)
    send_at = jnp.where(alive, bucket * 4 + spot, -1)

    kind = lax.broadcasted_iota(I32, (256, ROWS), 0)
    labels = jnp.where(kind < 128, (rank & 255).astype(F32), (clu & 1).astype(F32) + 2.0).astype(BF)
    own_lane = lax.broadcasted_iota(I32, (32, 8, 128), 2) == lax.broadcasted_iota(I32, (32, 8, 128), 1)

    @pl.loop(0, 4)
    def _(i):
        line = lax.broadcasted_iota(I32, (256, ROWS), 0) + i * 256
        where_to = jnp.where(line == send_at, 1.0, 0.0).astype(BF)
        code = mm(where_to, labels, NT)
        code = (code[:, :128] + 256.0 * code[:, 128:]).reshape(32, 8, 128)
        devs = pl.ds(pl.multiple_of(i * 32, 32), 32)
        tag_out[devs] = jnp.sum(jnp.where(own_lane, code, 0.0), axis=1, keepdims=True)

    def pack(f):
        @pl.loop(0, 2)
        def _(i):
            at = lax.broadcasted_iota(I32, (512, ROWS), 0)
            line = ((at >> 3) + i * 64) * 8 + f * 4 + (at & 3)
            where_to = jnp.where(line == send_at, 1.0, 0.0).astype(BF)
            front = (lax.broadcasted_iota(I32, (512, PART), 0) & 7) < 4
            rows = jnp.where(front, mm(where_to, unit[:, 0:PART]), mm(where_to, unit[:, PART:D]))
            packed[f, pl.ds(pl.multiple_of(i * 64, 64), 64)] = rows.reshape(64, 8, PART).astype(BF)

    def ship(src, dst, d, ssem, rsem):
        pltpu.make_async_remote_copy(
            src_ref=src, dst_ref=dst, send_sem=ssem, recv_sem=rsem,
            device_id=(lax.div(d, 16), lax.rem(d, 16)), device_id_type=MESH,
        ).start()

    pack(0)
    pl.semaphore_wait(barrier, DEVS - 1)

    pltpu.make_async_copy(tag_out.at[me], tag_in.at[me], recv5).start()
    pltpu.make_async_copy(packed.at[0, me], arrived.at[0, me], recv0.at[0]).start()

    @pl.loop(1, DEVS)
    def _(j):
        d = lax.rem(me + 37 * j, DEVS)
        ship(tag_out.at[d], tag_in.at[me], d, send5, recv5)
        ship(packed.at[0, d], arrived.at[0, me], d, send0.at[0], recv0.at[0])

    pack(1)
    pltpu.make_async_copy(packed.at[1, me], arrived.at[1, me], recv0.at[1]).start()

    @pl.loop(1, DEVS)
    def _(j):
        d = lax.rem(me + 37 * j, DEVS)
        ship(packed.at[1, d], arrived.at[1, me], d, send0.at[1], recv0.at[1])

    plan = []
    for p in range(2):
        block = pick(2 * k + p, FLAT_BLOCKS)
        turn = pick(2 * k + p, BLOCK_TURN)
        for a in range(8):
            other, c = pick(4 * block + a // 2, FLAT_SHARERS), a % 2
            pos = pick(4 * block + a // 2, FLAT_POS)
            plan.append((p, a, (other == k) & (mine_c == c), device_of(g, c, other), pos, turn))

    acc[...] = jnp.full(acc.shape, -1.0, F32)
    sub8 = lax.broadcasted_iota(I32, (DEVS, 8, 128), 1)
    lane8 = lax.broadcasted_iota(I32, (DEVS, 8, 128), 2)
    pltpu.make_async_copy(tag_in, tag_in, recv5).wait()

    lane = lax.broadcasted_iota(I32, (8, 128), 1)
    weigh = jnp.where(lane == 0, 1.0, jnp.where(lane == 1, 256.0, 0.0)).astype(BF)
    at_half = (lax.broadcasted_iota(I32, (1, ROWS), 1) >> 2) & 1
    lanes = lax.broadcasted_iota(I32, (ROWS, 128), 1)

    def tags(f):
        wide = jnp.broadcast_to(tag_in[...], (DEVS, 8, 128))
        wide = jnp.where(lane8 == f * 4 + (sub8 & 3), wide, 0.0)
        code = jnp.max(wide, axis=2, keepdims=True).reshape(ROWS, 1).astype(I32)
        both = jnp.where(lanes == 0, code & 255, jnp.where(lanes == 1, code >> 8, 0)).astype(F32).astype(BF)
        return mm(weigh, both, NT)[0:1, :].astype(I32) - 512

    slot_rows = [tags(f) for f in range(2)]
    first = lax.broadcasted_iota(I32, (256, 128), 1) == 0

    for f in range(2):
        pltpu.make_async_copy(arrived.at[f], arrived.at[f], recv0.at[f]).wait()
        got = arrived[f].reshape(ROWS, PART)
        for c in range(2):
            line = lax.broadcasted_iota(I32, (256, ROWS), 0) + c * 256
            front = jnp.where(line == jnp.where(at_half == 0, slot_rows[f], -1), 1.0, 0.0)
            rear = jnp.where(line == jnp.where(at_half == 1, slot_rows[f], -1), 1.0, 0.0)
            here = jnp.sum(front, axis=1, keepdims=True)
            rows = mm(front.astype(BF), got)
            split[2 * f + c, :, 0:128] = jnp.where(first & (here < 0.5), 256.0, rows[:, 0:128]).astype(BF)
            split[2 * f + c, :, 128:PART] = rows[:, 128:].astype(BF)
            split[2 * f + c, :, PART:D] = mm(rear.astype(BF), got).astype(BF)

        block = pick(2 * k + f, PHASE_BLOCK)
        turn = pick(2 * k + f, PHASE_TURN)
        slot = 2 * turn + mine_c
        to = held.at[pick(2 * k + f, PHASE_POS), slot]
        pltpu.make_async_copy(split.at[2 * f + mine_c], to, recv1.at[pick(2 * k + f, PHASE_POS), slot]).start()

        routes = []
        for step in range(4):
            t = lax.rem(turn + step, 4)
            other = pick(4 * block + t, FLAT_SHARERS)
            pos = pick(4 * block + t, FLAT_POS)
            for flip in range(2):
                if step or flip:
                    c = lax.rem(mine_c + flip, 2)
                    routes.append((step, flip, c, pos, goes(block, other, core), device_of(g, c, other)))

        @pl.loop(0, PIECES)
        def _(piece):
            rows = pl.ds(pl.multiple_of(piece * (HALF // PIECES), HALF // PIECES), HALF // PIECES)
            for step, flip, c, pos, wanted, device in routes:
                @pl.when(wanted)
                def _():
                    pltpu.make_async_remote_copy(
                        src_ref=split.at[2 * f + c, rows], dst_ref=held.at[pos, slot, rows],
                        send_sem=send1.at[2 * f + flip, step], recv_sem=recv1.at[pos, slot],
                        device_id=device, device_id_type=MESH,
                    ).start()

    diagonal = (k == 1) | (k == 7)
    both = (k < 2) | (k >= 6)
    probe = jnp.where(lax.broadcasted_iota(I32, (8, D), 1) == 0, 1.0, 0.0).astype(BF)

    def passes(p, s):
        owner = pick(4 * pick(2 * k + p, FLAT_BLOCKS) + lax.div(s, 2), FLAT_SHARERS)
        yes = lax.rem(owner, 2) == core
        return yes if p else yes & both

    def arrive(s):
        for p in range(2):
            pltpu.make_async_copy(held.at[p, s], held.at[p, s], recv1.at[p, s]).wait()

            @pl.when(passes(p, s))
            def _():
                pltpu.make_async_remote_copy(
                    src_ref=held.at[p, s], dst_ref=held.at[p, s], send_sem=send4.at[p, s], recv_sem=recv1.at[p, s],
                    device_id=(grp + 1 - 2 * core, mem), device_id_type=MESH,
                ).start()

        for p in range(2):
            mark = mm(probe, held[p, s], NT)[0:1, :]
            bias[p, s] = jnp.where(mark > 2.0, -1e4, 0.0)

    def compare(pr, lo, hi, pc, b, corner=False):
        n = hi - lo
        sims = mm(held[pr, lo:hi].reshape(n * 256, D), held[pc, b], NT) + bias[pc, b]
        if corner:
            below = lax.broadcasted_iota(I32, (n * 256, 256), 1) < lax.broadcasted_iota(I32, (n * 256, 256), 0)
            sims = jnp.where(below, sims, -1.0)
        sims = jnp.maximum(sims[:, :128], sims[:, 128:]).reshape(n, 256, 128)
        acc[pr, lo:hi] = jnp.maximum(acc[pr, lo:hi], sims)

    @pl.loop(0, 4)
    def _(s):
        arrive(s)

    @pl.when(jnp.logical_not(diagonal))
    def _():
        @pl.loop(0, 4)
        def _(b):
            compare(1, 0, 4, 0, b)

    @pl.when(diagonal)
    def _():
        @pl.loop(0, 2)
        def _(p):
            for b in range(4):
                compare(p, b, 4, p, b, True)

    @pl.loop(4, 8)
    def _(s):
        arrive(s)

    @pl.when(jnp.logical_not(diagonal))
    def _():
        for b in range(4):
            compare(1, 4, 8, 0, b)
        for b in range(4, 8):
            compare(1, 0, 8, 0, b)

    @pl.when(diagonal)
    def _():
        for p in range(2):
            for b in range(4):
                compare(p, 4, 8, p, b)
            for b in range(4, 8):
                compare(p, b, 8, p, b, True)

    def leave(p):
        for _, a, mine, device, pos, turn in plan[8 * p : 8 * p + 8]:
            pbest[p, a] = jnp.max(acc[p, a].T, axis=0, keepdims=True)

            @pl.when(mine)
            def _():
                to = rbest.at[pos, mine_c, turn]
                pltpu.make_async_copy(pbest.at[p, a], to, recv2.at[pos, mine_c, turn]).start()

            @pl.when(jnp.logical_not(mine))
            def _():
                pltpu.make_async_remote_copy(
                    src_ref=pbest.at[p, a], dst_ref=rbest.at[pos, mine_c, turn], send_sem=send2.at[p, a // 2, a % 2],
                    recv_sem=recv2.at[pos, mine_c, turn], device_id=device, device_id_type=MESH,
                ).start()

    def left(p):
        for _, a, mine, device, pos, turn in plan[8 * p : 8 * p + 8]:
            @pl.when(jnp.logical_not(mine))
            def _():
                pltpu.make_async_copy(pbest.at[p, a], pbest.at[p, a], send2.at[p, a // 2, a % 2]).wait()

    leave(1)
    pl.when(diagonal)(lambda: leave(0))

    sub = lax.broadcasted_iota(I32, (ROWS, 128), 0) & 7
    code = jnp.where(lane8 == sub8, jnp.broadcast_to(tag_in[...], (DEVS, 8, 128)), 0.0)
    code = jnp.max(code, axis=2, keepdims=True).reshape(ROWS, 1).astype(I32)
    slot_all = jnp.where(code >= 512, code - 512 + (sub >> 2) * 512, -1)

    @pl.loop(0, 16)
    def _(i):
        p, c, t = lax.div(i, 8), lax.rem(lax.div(i, 4), 2), lax.rem(i, 4)
        at = 4 * pick(2 * k + p, FLAT_BLOCKS) + t
        other = pick(at, FLAT_SHARERS)

        @pl.when((pick(at, FLAT_POS) == 1) | (other == 1) | (other == 7))
        def _():
            pltpu.make_async_copy(rbest.at[p, c, t], rbest.at[p, c, t], recv2.at[p, c, t]).wait()

    value = jnp.full((ROWS, 128), -1.0, F32)
    flipped = pick(2 * k, PHASE_POS) == 1
    for f in range(2):
        for c in range(2):
            best = jnp.where(flipped, jnp.max(rbest[1 - f, c], axis=0), jnp.max(rbest[f, c], axis=0))
            for e in range(2):
                at = lanes + (f * 512 + c * 256 + e * 128)
                value = jnp.where(slot_all == at, best[:, e * 128 : (e + 1) * 128], value)
    value = jnp.max(value, axis=1, keepdims=True)
    value = jnp.where(lanes == sub, value, -1.0).reshape(DEVS, 8, 128)
    rep[...] = jnp.max(value, axis=1, keepdims=True)

    pltpu.make_async_copy(rep.at[me], back.at[me], recv3).start()

    @pl.loop(1, DEVS)
    def _(j):
        d = lax.rem(me + 37 * j, DEVS)
        pltpu.make_async_remote_copy(
            src_ref=rep.at[d], dst_ref=back.at[me], send_sem=send3, recv_sem=recv3,
            device_id=(lax.div(d, 16), lax.rem(d, 16)), device_id_type=MESH,
        ).start()

    pltpu.make_async_copy(back, back, recv3).wait()
    mine = jnp.broadcast_to(back[...], (DEVS, 8, 128)).reshape(ROWS, 128)
    mine = jnp.max(jnp.where(lanes == sub, mine, -1.0), axis=1, keepdims=True)
    line = lax.broadcasted_iota(I32, (ROWS, 128), 0)
    for i in range(8):
        part = slice(i * 128, (i + 1) * 128)
        out_ref[:, part] = jnp.max(jnp.where(line == send_at[:, part], mine, -1.0), axis=0, keepdims=True)

    some = tag_out.at[pl.ds(0, DEVS - 1)]
    pltpu.make_async_copy(some, some, send5).wait()
    some = rep.at[pl.ds(0, DEVS - 1)]
    pltpu.make_async_copy(some, some, send3).wait()
    for f in range(2):
        some = packed.at[f, pl.ds(0, DEVS - 1)]
        pltpu.make_async_copy(some, some, send0.at[f]).wait()
        block = pick(2 * k + f, PHASE_BLOCK)
        turn = pick(2 * k + f, PHASE_TURN)
        for step in range(4):
            for flip in range(2):
                if step or flip:
                    other = pick(4 * block + lax.rem(turn + step, 4), FLAT_SHARERS)

                    @pl.when(goes(block, other, core))
                    def _():
                        pltpu.make_async_copy(split.at[0], split.at[0], send1.at[2 * f + flip, step]).wait()

        @pl.loop(0, 8)
        def _(s):
            @pl.when(passes(f, s))
            def _():
                pltpu.make_async_copy(held.at[f, s], held.at[f, s], send4.at[f, s]).wait()

    left(1)
    pl.when(diagonal)(lambda: left(0))


def on_device(embeddings, cluster, rank):
    vmem = pl.BlockSpec(memory_space=pltpu.VMEM)
    out = pl.pallas_call(
        kernel,
        out_shape=jax.ShapeDtypeStruct((1, ROWS), F32),
        in_specs=[vmem] * 3,
        out_specs=vmem,
        scratch_shapes=[
            pltpu.VMEM((ROWS, D), BF),
            pltpu.VMEM((2, DEVS, 8, PART), BF),
            pltpu.VMEM((2, DEVS, 8, PART), BF),
            pltpu.VMEM((DEVS, 1, 128), F32),
            pltpu.VMEM((DEVS, 1, 128), F32),
            pltpu.VMEM((4, HALF, D), BF),
            pltpu.VMEM((2, 8, HALF, D), BF),
            pltpu.VMEM((2, 8, HALF, 128), F32),
            pltpu.VMEM((2, 8, 1, HALF), F32),
            pltpu.VMEM((2, 2, 4, 1, HALF), F32),
            pltpu.VMEM((DEVS, 1, 128), F32),
            pltpu.VMEM((DEVS, 1, 128), F32),
            pltpu.VMEM((2, 8, 1, HALF), F32),
            pltpu.SemaphoreType.DMA((2,)),
            pltpu.SemaphoreType.DMA((2,)),
            pltpu.SemaphoreType.DMA((4, 4)),
            pltpu.SemaphoreType.DMA((2, 8)),
            pltpu.SemaphoreType.DMA((2, 4, 2)),
            pltpu.SemaphoreType.DMA((2, 2, 4)),
            pltpu.SemaphoreType.DMA,
            pltpu.SemaphoreType.DMA,
            pltpu.SemaphoreType.DMA((2, 8)),
            pltpu.SemaphoreType.DMA,
            pltpu.SemaphoreType.DMA,
        ],
        compiler_params=pltpu.CompilerParams(
            collective_id=0, has_side_effects=True, vmem_limit_bytes=56 * 2**20
        ),
        cost_estimate=pl.CostEstimate(flops=12_000_000_000, bytes_accessed=2_000_000, transcendentals=1024),
    )(embeddings, cluster.reshape(1, -1), rank.reshape(1, -1))
    return out.reshape(-1)


def solution(mesh):
    in_specs = (P(("grp", "mem"), None), P(("grp", "mem")), P(("grp", "mem")))
    out_specs = P(("grp", "mem"))
    return jax.shard_map(
        on_device, mesh=mesh, in_specs=in_specs, out_specs=out_specs, check_vma=False
    )
```

```python
import functools

import jax
import jax.numpy as jnp
from jax import lax
from jax.experimental import pallas as pl
from jax.experimental.pallas import tpu as pltpu
from jax.sharding import PartitionSpec as P

MESH = pl.DeviceIdType.MESH
D = 768
PART = 384
ROWS = 1024
HALF = 256
DEVS = 128
BF = jnp.bfloat16
F32 = jnp.float32
I32 = jnp.int32

BLOCKS = ((0, 1), (0, 1), (0, 2), (1, 2), (0, 3), (1, 3), (2, 3), (2, 3))
SHARERS = ((0, 2, 1, 4), (1, 3, 0, 5), (6, 7, 2, 3), (4, 5, 6, 7))
PLACE = ((1, 3, 3), (1, 2, 2), (1, 2, 3), (0, 1, 3), (1, 3, 2), (0, 2, 2), (0, 2, 3), (0, 1, 2))
SHIFTS = ((0, 0, 2), (1, 3, 0), (2, 2, 0))


def chip_of(spot, g):
    return tuple((PLACE[spot][a] + sum((g >> i & 1) * SHIFTS[i][a] for i in range(3))) % 4 for a in range(3))


CHIPS = {chip_of(spot, g): 8 * spot + g for spot in range(8) for g in range(8)}
WHO = [CHIPS[x, y, z] for x in range(4) for y in range(4) for z in range(4)]


def pick(index, table):
    out = jnp.int32(table[0])
    for at, value in enumerate(table):
        if at:
            out = jnp.where(index == at, jnp.int32(value), out)
    return out


def pick_vec(index, table):
    out = jnp.full_like(index, table[0])
    for at, value in enumerate(table):
        if at:
            out = jnp.where(index == at, jnp.int32(value), out)
    return out


def device_of(g, c, u):
    spot = 4 * c + lax.div(u, 2)
    bits = (lax.rem(g, 2), lax.rem(lax.div(g, 2), 2), lax.div(g, 4))
    x, y, z = (
        lax.rem(pick(spot, [p[a] for p in PLACE]) + sum(bits[i] * SHIFTS[i][a] for i in range(3)), 4) for a in range(3)
    )
    return 2 * x + lax.rem(u, 2), 4 * z + y


def my_place():
    grp, mem = lax.axis_index("grp"), lax.axis_index("mem")
    x, core = lax.div(grp, 2), lax.rem(grp, 2)
    z, y = lax.div(mem, 4), lax.rem(mem, 4)
    who = pick(16 * x + 4 * y + z, WHO)
    spot, g = lax.div(who, 8), lax.rem(who, 8)
    return grp, mem, g, lax.div(spot, 4), 2 * lax.rem(spot, 4) + core, core


FLAT_SHARERS = [k for row in SHARERS for k in row]
FLAT_POS = [BLOCKS[k].index(b) for b in range(4) for k in SHARERS[b]]
FLAT_BLOCKS = [b for pair in BLOCKS for b in pair]
PHASE_POS = [p for k in range(8) for p in sorted((0, 1), key=lambda p: SHARERS[BLOCKS[k][p]].index(k))]
PHASE_BLOCK = [BLOCKS[k][PHASE_POS[2 * k + f]] for k in range(8) for f in range(2)]
PHASE_TURN = [SHARERS[PHASE_BLOCK[2 * k + f]].index(k) for k in range(8) for f in range(2)]
BLOCK_TURN = [SHARERS[BLOCKS[k][p]].index(k) for k in range(8) for p in range(2)]
FLAT_PHASE = [t // 2 for b in range(4) for t in range(4)]

PIECES = 16
NT = (((1,), (1,)), ((), ()))
NN = (((1,), (0,)), ((), ()))


def mm(a, b, dims=NN):
    return lax.dot_general(a, b, dims, preferred_element_type=F32)


def goes(block, other, core):
    return (lax.rem(other, 2) == core) | ((block < 2) & (other >= 2))


def kernel(emb_ref, clu_ref, rank_ref, out_ref, unit, packed, arrived, tag_out, tag_in, split, held, acc, pbest,
           rbest, rep, back, bias, send0, recv0, send1, recv1, send2, recv2, send3, recv3, send4, send5, recv5):
    grp, mem, g, mine_c, k, core = my_place()
    me = grp * 16 + mem
    rbest[...] = jnp.full(rbest.shape, -1.0, F32)

    barrier = pltpu.get_barrier_semaphore()

    @pl.loop(1, DEVS)
    def _(j):
        d = lax.rem(me + j, DEVS)
        pl.semaphore_signal(barrier, inc=1, device_id=(lax.div(d, 16), lax.rem(d, 16)), device_id_type=MESH)

    @pl.loop(0, 4)
    def _(i):
        rows = pl.ds(pl.multiple_of(i * 256, 256), 256)
        wide = emb_ref[rows, :].astype(F32)
        total = jnp.sum(wide * wide, axis=1, keepdims=True)
        unit[rows, :] = (wide * lax.rsqrt(total + 1e-06)).astype(BF)

    clu, rank = clu_ref[...], rank_ref[...]
    alive = clu >= 0
    vg = clu >> 1
    vh = rank >> 8
    share = ((vh >> 3) << 2) + ((vh & 7) >> 1)
    vk = pick_vec(share, FLAT_SHARERS)
    vp = pick_vec(share, FLAT_PHASE)
    vs = 4 * (vh & 1) + (vk >> 1)
    vx, vy, vz = (
        (pick_vec(vs, [p[a] for p in PLACE]) + sum((vg >> i & 1) * SHIFTS[i][a] for i in range(3))) & 3 for a in range(3)
    )
    vdev = (2 * vx + (vk & 1)) * 16 + 4 * vz + vy
    bucket = jnp.where(alive, 2 * vdev + vp, -1)
    low = lax.broadcasted_iota(I32, (128, 256), 0)
    col = lax.broadcasted_iota(I32, (128, 256), 1)
    tri = jnp.where((low < col) | (col >= 128), 1.0, 0.0).astype(BF)
    carry = jnp.zeros((256, 128), F32)
    bid = lax.broadcasted_iota(I32, (256, 128), 0)
    spots = []
    for i in range(8):
        hit = bid == bucket[:, i * 128 : (i + 1) * 128]
        counts = mm(jnp.where(hit, 1.0, 0.0).astype(BF), tri)
        spots.append(jnp.sum(jnp.where(hit, counts[:, :128] + carry, 0.0), axis=0, keepdims=True))
        carry = carry + counts[:, 128:]
    spot = jnp.concatenate(spots, axis=1).astype(I32)
    send_at = jnp.where(alive, bucket * 4 + spot, -1)

    kind = lax.broadcasted_iota(I32, (256, ROWS), 0)
    labels = jnp.where(kind < 128, (rank & 255).astype(F32), (clu & 1).astype(F32) + 2.0).astype(BF)
    own_lane = lax.broadcasted_iota(I32, (32, 8, 128), 2) == lax.broadcasted_iota(I32, (32, 8, 128), 1)

    @pl.loop(0, 4)
    def _(i):
        line = lax.broadcasted_iota(I32, (256, ROWS), 0) + i * 256
        where_to = jnp.where(line == send_at, 1.0, 0.0).astype(BF)
        code = mm(where_to, labels, NT)
        code = (code[:, :128] + 256.0 * code[:, 128:]).reshape(32, 8, 128)
        devs = pl.ds(pl.multiple_of(i * 32, 32), 32)
        tag_out[devs] = jnp.sum(jnp.where(own_lane, code, 0.0), axis=1, keepdims=True)

    def pack(f):
        @pl.loop(0, 2)
        def _(i):
            at = lax.broadcasted_iota(I32, (512, ROWS), 0)
            line = ((at >> 3) + i * 64) * 8 + f * 4 + (at & 3)
            where_to = jnp.where(line == send_at, 1.0, 0.0).astype(BF)
            front = (lax.broadcasted_iota(I32, (512, PART), 0) & 7) < 4
            rows = jnp.where(front, mm(where_to, unit[:, 0:PART]), mm(where_to, unit[:, PART:D]))
            packed[f, pl.ds(pl.multiple_of(i * 64, 64), 64)] = rows.reshape(64, 8, PART).astype(BF)

    def ship(src, dst, d, ssem, rsem):
        pltpu.make_async_remote_copy(
            src_ref=src, dst_ref=dst, send_sem=ssem, recv_sem=rsem,
            device_id=(lax.div(d, 16), lax.rem(d, 16)), device_id_type=MESH,
        ).start()

    pack(0)
    pl.semaphore_wait(barrier, DEVS - 1)

    pltpu.make_async_copy(tag_out.at[me], tag_in.at[me], recv5).start()
    pltpu.make_async_copy(packed.at[0, me], arrived.at[0, me], recv0.at[0]).start()

    @pl.loop(1, DEVS)
    def _(j):
        d = lax.rem(me + 37 * j, DEVS)
        ship(tag_out.at[d], tag_in.at[me], d, send5, recv5)
        ship(packed.at[0, d], arrived.at[0, me], d, send0.at[0], recv0.at[0])

    pack(1)
    pltpu.make_async_copy(packed.at[1, me], arrived.at[1, me], recv0.at[1]).start()

    @pl.loop(1, DEVS)
    def _(j):
        d = lax.rem(me + 37 * j, DEVS)
        ship(packed.at[1, d], arrived.at[1, me], d, send0.at[1], recv0.at[1])

    plan = []
    for p in range(2):
        block = pick(2 * k + p, FLAT_BLOCKS)
        turn = pick(2 * k + p, BLOCK_TURN)
        for a in range(8):
            other, c = pick(4 * block + a // 2, FLAT_SHARERS), a % 2
            pos = pick(4 * block + a // 2, FLAT_POS)
            plan.append((p, a, (other == k) & (mine_c == c), device_of(g, c, other), pos, turn))

    acc[...] = jnp.full(acc.shape, -1.0, F32)
    sub8 = lax.broadcasted_iota(I32, (DEVS, 8, 128), 1)
    lane8 = lax.broadcasted_iota(I32, (DEVS, 8, 128), 2)
    pltpu.make_async_copy(tag_in, tag_in, recv5).wait()

    lane = lax.broadcasted_iota(I32, (8, 128), 1)
    weigh = jnp.where(lane == 0, 1.0, jnp.where(lane == 1, 256.0, 0.0)).astype(BF)
    at_half = (lax.broadcasted_iota(I32, (1, ROWS), 1) >> 2) & 1
    lanes = lax.broadcasted_iota(I32, (ROWS, 128), 1)

    def tags(f):
        wide = jnp.broadcast_to(tag_in[...], (DEVS, 8, 128))
        wide = jnp.where(lane8 == f * 4 + (sub8 & 3), wide, 0.0)
        code = jnp.max(wide, axis=2, keepdims=True).reshape(ROWS, 1).astype(I32)
        both = jnp.where(lanes == 0, code & 255, jnp.where(lanes == 1, code >> 8, 0)).astype(F32).astype(BF)
        return mm(weigh, both, NT)[0:1, :].astype(I32) - 512

    slot_rows = [tags(f) for f in range(2)]
    first = lax.broadcasted_iota(I32, (256, 128), 1) == 0

    for f in range(2):
        pltpu.make_async_copy(arrived.at[f], arrived.at[f], recv0.at[f]).wait()
        got = arrived[f].reshape(ROWS, PART)
        for c in range(2):
            line = lax.broadcasted_iota(I32, (256, ROWS), 0) + c * 256
            front = jnp.where(line == jnp.where(at_half == 0, slot_rows[f], -1), 1.0, 0.0)
            rear = jnp.where(line == jnp.where(at_half == 1, slot_rows[f], -1), 1.0, 0.0)
            here = jnp.sum(front, axis=1, keepdims=True)
            rows = mm(front.astype(BF), got)
            split[2 * f + c, :, 0:128] = jnp.where(first & (here < 0.5), 256.0, rows[:, 0:128]).astype(BF)
            split[2 * f + c, :, 128:PART] = rows[:, 128:].astype(BF)
            split[2 * f + c, :, PART:D] = mm(rear.astype(BF), got).astype(BF)

        block = pick(2 * k + f, PHASE_BLOCK)
        turn = pick(2 * k + f, PHASE_TURN)
        slot = 2 * turn + mine_c
        to = held.at[pick(2 * k + f, PHASE_POS), slot]
        pltpu.make_async_copy(split.at[2 * f + mine_c], to, recv1.at[pick(2 * k + f, PHASE_POS), slot]).start()

        routes = []
        for step in range(4):
            t = lax.rem(turn + step, 4)
            other = pick(4 * block + t, FLAT_SHARERS)
            pos = pick(4 * block + t, FLAT_POS)
            for flip in range(2):
                if step or flip:
                    c = lax.rem(mine_c + flip, 2)
                    routes.append((step, flip, c, pos, goes(block, other, core), device_of(g, c, other)))

        @pl.loop(0, PIECES)
        def _(piece):
            rows = pl.ds(pl.multiple_of(piece * (HALF // PIECES), HALF // PIECES), HALF // PIECES)
            for step, flip, c, pos, wanted, device in routes:
                @pl.when(wanted)
                def _():
                    pltpu.make_async_remote_copy(
                        src_ref=split.at[2 * f + c, rows], dst_ref=held.at[pos, slot, rows],
                        send_sem=send1.at[2 * f + flip, step], recv_sem=recv1.at[pos, slot],
                        device_id=device, device_id_type=MESH,
                    ).start()

    diagonal = (k == 1) | (k == 7)
    both = (k < 2) | (k >= 6)
    probe = jnp.where(lax.broadcasted_iota(I32, (8, D), 1) == 0, 1.0, 0.0).astype(BF)

    def passes(p, s):
        owner = pick(4 * pick(2 * k + p, FLAT_BLOCKS) + lax.div(s, 2), FLAT_SHARERS)
        yes = lax.rem(owner, 2) == core
        return yes if p else yes & both

    def arrive(s):
        for p in range(2):
            pltpu.make_async_copy(held.at[p, s], held.at[p, s], recv1.at[p, s]).wait()

            @pl.when(passes(p, s))
            def _():
                pltpu.make_async_remote_copy(
                    src_ref=held.at[p, s], dst_ref=held.at[p, s], send_sem=send4.at[p, s], recv_sem=recv1.at[p, s],
                    device_id=(grp + 1 - 2 * core, mem), device_id_type=MESH,
                ).start()

    def note(s):
        for p in range(2):
            mark = mm(probe, held[p, s], NT)[0:1, :]
            bias[p, s] = jnp.where(mark > 2.0, -1e4, 0.0)

    def compare(pr, lo, hi, pc, b, corner=False):
        n = hi - lo
        sims = mm(held[pr, lo:hi].reshape(n * 256, D), held[pc, b], NT) + bias[pc, b]
        if corner:
            below = lax.broadcasted_iota(I32, (n * 256, 256), 1) < lax.broadcasted_iota(I32, (n * 256, 256), 0)
            sims = jnp.where(below, sims, -1.0)
        sims = jnp.maximum(sims[:, :128], sims[:, 128:]).reshape(n, 256, 128)
        acc[pr, lo:hi] = jnp.maximum(acc[pr, lo:hi], sims)

    @pl.loop(0, 4)
    def _(s):
        arrive(s)

    @pl.loop(0, 4)
    def _(s):
        note(s)

    @pl.when(jnp.logical_not(diagonal))
    def _():
        @pl.loop(0, 4)
        def _(b):
            compare(1, 0, 4, 0, b)

    @pl.when(diagonal)
    def _():
        @pl.loop(0, 2)
        def _(p):
            for b in range(4):
                compare(p, b, 4, p, b, True)

    @pl.loop(4, 8)
    def _(s):
        arrive(s)

    for s in range(4, 8):
        note(s)

    @pl.when(jnp.logical_not(diagonal))
    def _():
        for b in range(4):
            compare(1, 4, 8, 0, b)
        for b in range(4, 8):
            compare(1, 0, 8, 0, b)

    @pl.when(diagonal)
    def _():
        for p in range(2):
            for b in range(4):
                compare(p, 4, 8, p, b)
            for b in range(4, 8):
                compare(p, b, 8, p, b, True)

    def leave(p):
        for _, a, mine, device, pos, turn in plan[8 * p : 8 * p + 8]:
            pbest[p, a] = jnp.max(acc[p, a].T, axis=0, keepdims=True)

            @pl.when(mine)
            def _():
                to = rbest.at[pos, mine_c, turn]
                pltpu.make_async_copy(pbest.at[p, a], to, recv2.at[pos, mine_c, turn]).start()

            @pl.when(jnp.logical_not(mine))
            def _():
                pltpu.make_async_remote_copy(
                    src_ref=pbest.at[p, a], dst_ref=rbest.at[pos, mine_c, turn], send_sem=send2.at[p, a // 2, a % 2],
                    recv_sem=recv2.at[pos, mine_c, turn], device_id=device, device_id_type=MESH,
                ).start()

    def left(p):
        for _, a, mine, device, pos, turn in plan[8 * p : 8 * p + 8]:
            @pl.when(jnp.logical_not(mine))
            def _():
                pltpu.make_async_copy(pbest.at[p, a], pbest.at[p, a], send2.at[p, a // 2, a % 2]).wait()

    leave(1)
    pl.when(diagonal)(lambda: leave(0))

    sub = lax.broadcasted_iota(I32, (ROWS, 128), 0) & 7
    code = jnp.where(lane8 == sub8, jnp.broadcast_to(tag_in[...], (DEVS, 8, 128)), 0.0)
    code = jnp.max(code, axis=2, keepdims=True).reshape(ROWS, 1).astype(I32)
    slot_all = jnp.where(code >= 512, code - 512 + (sub >> 2) * 512, -1)

    @pl.loop(0, 16)
    def _(i):
        p, c, t = lax.div(i, 8), lax.rem(lax.div(i, 4), 2), lax.rem(i, 4)
        at = 4 * pick(2 * k + p, FLAT_BLOCKS) + t
        other = pick(at, FLAT_SHARERS)

        @pl.when((pick(at, FLAT_POS) == 1) | (other == 1) | (other == 7))
        def _():
            pltpu.make_async_copy(rbest.at[p, c, t], rbest.at[p, c, t], recv2.at[p, c, t]).wait()

    value = jnp.full((ROWS, 128), -1.0, F32)
    flipped = pick(2 * k, PHASE_POS) == 1
    for f in range(2):
        for c in range(2):
            best = jnp.where(flipped, jnp.max(rbest[1 - f, c], axis=0), jnp.max(rbest[f, c], axis=0))
            for e in range(2):
                at = lanes + (f * 512 + c * 256 + e * 128)
                value = jnp.where(slot_all == at, best[:, e * 128 : (e + 1) * 128], value)
    value = jnp.max(value, axis=1, keepdims=True)
    value = jnp.where(lanes == sub, value, -1.0).reshape(DEVS, 8, 128)
    rep[...] = jnp.max(value, axis=1, keepdims=True)

    pltpu.make_async_copy(rep.at[me], back.at[me], recv3).start()

    @pl.loop(1, DEVS)
    def _(j):
        d = lax.rem(me + 37 * j, DEVS)
        pltpu.make_async_remote_copy(
            src_ref=rep.at[d], dst_ref=back.at[me], send_sem=send3, recv_sem=recv3,
            device_id=(lax.div(d, 16), lax.rem(d, 16)), device_id_type=MESH,
        ).start()

    pltpu.make_async_copy(back, back, recv3).wait()
    mine = jnp.broadcast_to(back[...], (DEVS, 8, 128)).reshape(ROWS, 128)
    mine = jnp.max(jnp.where(lanes == sub, mine, -1.0), axis=1, keepdims=True)
    line = lax.broadcasted_iota(I32, (ROWS, 128), 0)
    for i in range(8):
        part = slice(i * 128, (i + 1) * 128)
        out_ref[:, part] = jnp.max(jnp.where(line == send_at[:, part], mine, -1.0), axis=0, keepdims=True)

    some = tag_out.at[pl.ds(0, DEVS - 1)]
    pltpu.make_async_copy(some, some, send5).wait()
    some = rep.at[pl.ds(0, DEVS - 1)]
    pltpu.make_async_copy(some, some, send3).wait()
    for f in range(2):
        some = packed.at[f, pl.ds(0, DEVS - 1)]
        pltpu.make_async_copy(some, some, send0.at[f]).wait()
        block = pick(2 * k + f, PHASE_BLOCK)
        turn = pick(2 * k + f, PHASE_TURN)
        for step in range(4):
            for flip in range(2):
                if step or flip:
                    other = pick(4 * block + lax.rem(turn + step, 4), FLAT_SHARERS)

                    @pl.when(goes(block, other, core))
                    def _():
                        pltpu.make_async_copy(split.at[0], split.at[0], send1.at[2 * f + flip, step]).wait()

        @pl.loop(0, 8)
        def _(s):
            @pl.when(passes(f, s))
            def _():
                pltpu.make_async_copy(held.at[f, s], held.at[f, s], send4.at[f, s]).wait()

    left(1)
    pl.when(diagonal)(lambda: left(0))


def on_device(embeddings, cluster, rank):
    vmem = pl.BlockSpec(memory_space=pltpu.VMEM)
    out = pl.pallas_call(
        kernel,
        out_shape=jax.ShapeDtypeStruct((1, ROWS), F32),
        in_specs=[vmem] * 3,
        out_specs=vmem,
        scratch_shapes=[
            pltpu.VMEM((ROWS, D), BF),
            pltpu.VMEM((2, DEVS, 8, PART), BF),
            pltpu.VMEM((2, DEVS, 8, PART), BF),
            pltpu.VMEM((DEVS, 1, 128), F32),
            pltpu.VMEM((DEVS, 1, 128), F32),
            pltpu.VMEM((4, HALF, D), BF),
            pltpu.VMEM((2, 8, HALF, D), BF),
            pltpu.VMEM((2, 8, HALF, 128), F32),
            pltpu.VMEM((2, 8, 1, HALF), F32),
            pltpu.VMEM((2, 2, 4, 1, HALF), F32),
            pltpu.VMEM((DEVS, 1, 128), F32),
            pltpu.VMEM((DEVS, 1, 128), F32),
            pltpu.VMEM((2, 8, 1, HALF), F32),
            pltpu.SemaphoreType.DMA((2,)),
            pltpu.SemaphoreType.DMA((2,)),
            pltpu.SemaphoreType.DMA((4, 4)),
            pltpu.SemaphoreType.DMA((2, 8)),
            pltpu.SemaphoreType.DMA((2, 4, 2)),
            pltpu.SemaphoreType.DMA((2, 2, 4)),
            pltpu.SemaphoreType.DMA,
            pltpu.SemaphoreType.DMA,
            pltpu.SemaphoreType.DMA((2, 8)),
            pltpu.SemaphoreType.DMA,
            pltpu.SemaphoreType.DMA,
        ],
        compiler_params=pltpu.CompilerParams(
            collective_id=0, has_side_effects=True, vmem_limit_bytes=56 * 2**20
        ),
        cost_estimate=pl.CostEstimate(flops=12_000_000_000, bytes_accessed=2_000_000, transcendentals=1024),
    )(embeddings, cluster.reshape(1, -1), rank.reshape(1, -1))
    return out.reshape(-1)


def solution(mesh):
    in_specs = (P(("grp", "mem"), None), P(("grp", "mem")), P(("grp", "mem")))
    out_specs = P(("grp", "mem"))
    return jax.shard_map(
        on_device, mesh=mesh, in_specs=in_specs, out_specs=out_specs, check_vma=False
    )
```
